32 devices in a mesh: row: 4 (over y, x), col: 4 (over z), rep: 2 (over core).
Axes of the slice: x: 2, y: 2, z: 4, core: 2. Of those that a mesh axis runs over, the one named last changes fastest.
Arguments:
- amplitudes: bfloat16 [16, 16, 6, 5184], P('row', 'col', 'rep'), may hold values from -6 to 6
- integrals: bfloat16 [5184, 6, 5184], P('col', 'rep', 'row'), may hold values from -0.03125 to 0.03125
- occ_offsets: int32 [9], replicated, may hold values from 0 to 16, as said below
- slab: int32 [2], replicated, may hold values from 0 to 7
Outputs:
- residual: bfloat16 [16, 16, 5184], P('row', 'col')
The draws below stay inside these ranges and needn't reach their ends.
Inputs may be any that keep to these rules, and one draw needn't show every extreme that they name: `occ_offsets`: never falling; entry 0 is 0 and entry 8 is 16; entries k and k+1 bound the occupied orbitals of irrep k.
All inputs are finite; a program needn't handle non-finite values.
Results may differ from the reference program's by a relative error of at most 0.02.
Values may be sent and summed in bfloat16 or wider, within the bound.
A program may use at most 128 MiB of HBM per device.

```python
import jax
import jax.numpy as jnp
from jax import lax

KB = 6
O = 16
CDB = 5184
AB = 5184
N_ROW = 4
N_REP = 2


def draw_occ_offsets(key, part):
    inner = jnp.sort(jax.random.randint(key, (7,), 0, O + 1)).astype(jnp.int32)
    first = jnp.zeros((1,), jnp.int32)
    last = jnp.full((1,), O, jnp.int32)
    return jnp.concatenate([first, inner, last])


def steps_of(stream_key, shape, pieces, smallest, high):
    gain, own = 1.0, jax.random.fold_in(stream_key, 6)
    for dim, parts in pieces:
        steps = jnp.exp(jax.random.uniform(jax.random.fold_in(own, dim), (parts,), jnp.float32, smallest / len(pieces), high / len(pieces)))
        gain = gain * jnp.repeat(steps, shape[dim] // parts).reshape([-1 if axis == dim else 1 for axis in range(len(shape))])
    return gain


def normal_values(rng, shape, spread, reach, shards=(), kind=jnp.bfloat16):
    drawn = spread * jax.random.normal(rng, shape, jnp.float32)
    if shards:
        drawn = drawn * steps_of(rng, shape, shards, -0.22, 0.18)
    return jnp.clip(drawn, -reach, reach).astype(kind)


def setup_inputs(seed: int = 0) -> dict:
    arg_keys = jax.random.split(jax.random.key(seed), 5)
    amplitudes = normal_values(arg_keys[0], (O, O, KB, CDB), 1.0, 6.0, ((0, 4), (1, 4), (2, 2)))
    integrals = normal_values(arg_keys[1], (AB, KB, CDB), (KB * CDB) ** -0.5, 0.03125, ((0, 4), (1, 2), (2, 4)))
    occ_offsets = draw_occ_offsets(jax.random.fold_in(arg_keys[4], 71), 0)
    slab = jax.random.randint(arg_keys[3], (2,), 0, 8).astype(jnp.int32)
    return dict(amplitudes=amplitudes, integrals=integrals, occ_offsets=occ_offsets, slab=slab)


def irrep_labels(orbitals, occ_offsets):
    return jnp.sum((orbitals[:, None] >= occ_offsets[None, 1:8]).astype(jnp.int32), axis=1).astype(jnp.int32)


def reference(amplitudes, integrals, occ_offsets, slab):
    half_blocks = KB // N_REP
    sub_width = CDB // N_ROW
    blocked_amps = amplitudes.reshape(O, O, N_REP, half_blocks, N_ROW, sub_width)
    blocked_ints = integrals.reshape(AB, N_REP, half_blocks, N_ROW, sub_width)

    def accumulate(total, number):
        rep_part = number // N_ROW
        row_part = number % N_ROW
        amps = lax.dynamic_index_in_dim(blocked_amps, rep_part, 2, keepdims=False)
        amps = lax.dynamic_index_in_dim(amps, row_part, 3, keepdims=False)
        ints = lax.dynamic_index_in_dim(blocked_ints, rep_part, 1, keepdims=False)
        ints = lax.dynamic_index_in_dim(ints, row_part, 2, keepdims=False)
        partial_value = jnp.einsum('ijkc,akc->ija', amps.astype(jnp.float32), ints.astype(jnp.float32))
        rounded = lax.optimization_barrier(partial_value.astype(jnp.bfloat16))
        return total + rounded.astype(jnp.float32), None

    numbers = jnp.arange(N_REP * N_ROW, dtype=jnp.int32)
    total = lax.scan(accumulate, jnp.zeros((O, O, AB), jnp.float32), numbers)[0]
    ladder = lax.optimization_barrier(total.astype(jnp.bfloat16))
    orbitals = jnp.arange(O, dtype=jnp.int32)
    labels = irrep_labels(orbitals, occ_offsets)
    target = jnp.bitwise_xor(slab[0], slab[1])
    allowed = jnp.bitwise_xor(labels[:, None], labels[None, :]) == target
    wide = ladder.astype(jnp.float32)
    mixed = wide - jnp.swapaxes(wide, 0, 1)
    return jnp.where(allowed[:, :, None], mixed, jnp.float32(0.0)).astype(jnp.bfloat16)
```

```python
import jax
import jax.numpy as jnp
from jax import lax
from jax.sharding import PartitionSpec as P


def irrep_labels(orbitals, occ_offsets):
    return jnp.sum((orbitals[:, None] >= occ_offsets[None, 1:8]).astype(jnp.int32), axis=1)


def shards(amplitudes, integrals, occ_offsets, slab):
    block_rows, block_cols = amplitudes.shape[:2]
    shuffled = lax.all_to_all(amplitudes, "row", split_axis=3, concat_axis=0, tiled=True)
    amps = lax.all_gather(shuffled, "col", axis=1, tiled=True)
    partial = jnp.einsum("ijkc,akc->ija", amps, integrals, preferred_element_type=jnp.float32)
    mixed = (partial - jnp.swapaxes(partial, 0, 1)).astype(jnp.bfloat16)
    summed = lax.psum_scatter(mixed, ("row", "rep"), scatter_dimension=0, tiled=True)
    summed = lax.all_to_all(summed, "col", split_axis=1, concat_axis=2, tiled=True)
    ladder = lax.all_gather(summed, "rep", axis=0, tiled=True)
    row_orbitals = lax.axis_index("row") * block_rows + jnp.arange(block_rows, dtype=jnp.int32)
    col_orbitals = lax.axis_index("col") * block_cols + jnp.arange(block_cols, dtype=jnp.int32)
    target = jnp.bitwise_xor(slab[0], slab[1])
    row_labels = irrep_labels(row_orbitals, occ_offsets)
    col_labels = irrep_labels(col_orbitals, occ_offsets)
    allowed = jnp.bitwise_xor(row_labels[:, None], col_labels[None, :]) == target
    return jnp.where(allowed[:, :, None], ladder, jnp.bfloat16(0.0))


def solution(mesh):
    placed = (P("row", "col", "rep", None), P("col", "rep", "row"), P(), P())
    return jax.shard_map(
        shards, mesh=mesh, in_specs=placed, out_specs=P("row", "col", None), check_vma=False
    )
```

```python
import functools

import jax
import jax.numpy as jnp
from jax import lax
from jax.experimental import pallas as pl
from jax.experimental.pallas import tpu as pltpu
from jax.sharding import PartitionSpec as P

MESH = pl.DeviceIdType.MESH


def irrep_labels(orbitals, occ_offsets):
    return jnp.sum((orbitals[:, None] >= occ_offsets[None, 1:8]).astype(jnp.int32), axis=1)


def pair_start(first, n):
    return first * n - first * (first - 1) // 2


def kernel(n, reps, s_ref, v_hbm, out_ref, x, dd, v, acc, pb, rrecv, qb, rowrecv, res,
           lv, a_send, a_recv, l_send, r_send, x_recv, p_send, p_recv, q_send, q_recv,
           o_send, o_recv):
    kb = s_ref.shape[1]
    per_rep = pb.shape[1]
    slots = res.shape[0]
    r, z, p = lax.axis_index("row"), lax.axis_index("col"), lax.axis_index("rep")

    def remote(src, dst, send, recv, **where):
        target = {"row": r, "col": z, "rep": p, **where}
        return pltpu.make_async_remote_copy(
            src_ref=src, dst_ref=dst, send_sem=send, recv_sem=recv,
            device_id=(target["row"], target["col"], target["rep"]), device_id_type=MESH)

    for k in range(kb):
        pltpu.make_async_copy(v_hbm.at[k], v.at[k], lv.at[k]).start()

    barrier = pltpu.get_barrier_semaphore()
    devices = n * n * reps
    me = (r * n + z) * reps + p

    @pl.loop(1, devices)
    def _(off):
        other = lax.rem(me + off, devices)
        pl.semaphore_signal(
            barrier, inc=1,
            device_id=(other // (n * reps), lax.rem(other // reps, n), lax.rem(other, reps)),
            device_id_type=MESH)

    pl.semaphore_wait(barrier, devices - 1)

    def shuffle(k, off):
        dest = lax.rem(r + off, n)
        return remote(s_ref.at[dest, k], x.at[k, z, r], a_send.at[k, off - 1],
                      a_recv.at[k, off - 1], row=dest)

    def shuffled(k, off):
        source = lax.rem(r + n - off, n)
        return remote(s_ref.at[source, k], x.at[k, z, source], a_send.at[k, off - 1],
                      a_recv.at[k, off - 1], row=source)

    for k in range(kb):
        for off in range(1, n):
            shuffle(k, off).start()
        x[k, z, r] = s_ref[r, k]
    acc[...] = jnp.zeros_like(acc)
    if reps * per_rep != n * (n + 1) // 2:
        dd[...] = jnp.zeros_like(dd)

    def to_left(k, c):
        part = x.at[k, c, pl.ds(0, c + 1)]
        return remote(part, part, l_send.at[k, c], x_recv.at[k, c], col=lax.max(z - 1, 0))

    def to_right(k, c):
        part = x.at[k, c, pl.ds(c, n - c)]
        return remote(part, part, r_send.at[k, c], x_recv.at[k, c], col=lax.min(z + 1, n - 1))

    for k in range(kb):
        for off in range(1, n):
            shuffled(k, off).wait_recv()
        for c in range(n):
            @pl.when(z == c)
            def _():
                if c > 0:
                    to_left(k, c).start()
                if c < n - 1:
                    to_right(k, c).start()

    def assemble(k, first, second):
        number = pair_start(first, n) + second - first
        slot = lax.rem(number, reps) * per_rep + number // reps

        @pl.when(z <= first)
        def _():
            dd[slot] = x[k, second, first]

        @pl.when((z >= second) & (z > first))
        def _():
            dd[slot] = x[k, first, second]

        @pl.when((z > first) & (z < second))
        def _():
            dd[slot] = (x[k, second, first].astype(jnp.float32)
                        - x[k, first, second].astype(jnp.float32)).astype(dd.dtype)

    def arrivals(k, d):
        for c in range(n):
            if c >= d:
                @pl.when(z == c - d)
                def _():
                    to_left(k, c).wait_recv()
                    x[k, c, c - d] = (x[k, c, c - d].astype(jnp.float32)
                                      - x[k, c - d, c].astype(jnp.float32)).astype(x.dtype)
                    if c > d:
                        to_left(k, c).start()
            if c + d < n:
                @pl.when(z == c + d)
                def _():
                    to_right(k, c).wait_recv()
                    x[k, c, c + d] = (x[k, c + d, c].astype(jnp.float32)
                                      - x[k, c, c + d].astype(jnp.float32)).astype(x.dtype)
                    if c + d < n - 1:
                        to_right(k, c).start()

    for d in range(1, n):
        @pl.loop(0, kb)
        def _(k):
            arrivals(k, d)
            if d == n - 1:
                @pl.loop(0, n)
                def _(first):
                    @pl.loop(first, n)
                    def _(second):
                        assemble(k, first, second)

                pltpu.make_async_copy(v_hbm.at[k], v.at[k], lv.at[k]).wait()
                acc[...] += lax.dot_general(
                    dd[...].reshape(acc.shape[0], dd.shape[2]), v[k],
                    (((1,), (1,)), ((), ())), preferred_element_type=jnp.float32)

    pb[...] = acc[...].reshape(pb.shape).astype(pb.dtype)

    def swap_reps(off):
        other = lax.rem(p + off, reps)
        return remote(pb.at[other], rrecv.at[off - 1], p_send.at[off - 1], p_recv.at[off - 1],
                      rep=other)

    for off in range(1, reps):
        swap_reps(off).start()
    for off in range(1, reps):
        swap_reps(off).wait_recv()

    flip = lax.rem(p, 2)

    def owner(q):
        return lax.rem(q, n) * (1 - 2 * flip) + (n - 1) * flip

    def to_owner(q):
        return remote(qb.at[q], rowrecv.at[q // n, r], q_send.at[q],
                      q_recv.at[q // n, r], row=owner(q))

    for q in range(per_rep):
        total = pb[p, q].astype(jnp.float32)
        for off in range(1, reps):
            total += rrecv[off - 1, q].astype(jnp.float32)
        qb[q] = total.astype(qb.dtype)

        @pl.when(owner(q) != r)
        def _():
            to_owner(q).start()

    mine = r * (1 - 2 * flip) + (n - 1) * flip

    def deliver(s, do):
        number = (s * n + mine) * reps + p
        first = 0
        for t in range(1, n):
            first = first + (number >= pair_start(t, n)).astype(jnp.int32)
        second = number - pair_start(first, n) + first
        for rep in range(reps):
            for t, (row, col) in enumerate(((first, second), (second, first))):
                local = (row == r) & (col == z) & (p == rep)
                wanted = (first != second) if t else (first == first)

                @pl.when(wanted & local)
                def _():
                    if do == "start":
                        pltpu.make_async_copy(res.at[s], out_ref.at[z], o_recv.at[z]).start()

                @pl.when(wanted & jnp.logical_not(local))
                def _():
                    copy = remote(res.at[s], out_ref.at[z], o_send.at[s, rep, t], o_recv.at[z],
                                  row=row, col=col, rep=rep)
                    if do == "start":
                        copy.start()
                    else:
                        copy.wait_send()

    for s in range(slots):
        @pl.when(s * n + mine < per_rep)
        def _():
            total = qb[s * n + mine].astype(jnp.float32)
            for off in range(1, n):
                source = lax.rem(r + off, n)
                remote(rowrecv.at[s, source], rowrecv.at[s, source], q_send.at[0],
                       q_recv.at[s, source], row=source).wait_recv()
                total += rowrecv[s, source].astype(jnp.float32)
            res[s] = total.astype(res.dtype)
            deliver(s, "start")

    for source in range(n):
        remote(out_ref.at[source], out_ref.at[source], o_send.at[0, 0, 0], o_recv.at[source],
               col=source).wait_recv()

    for s in range(slots):
        @pl.when(s * n + mine < per_rep)
        def _():
            deliver(s, "wait")
    for q in range(per_rep):
        @pl.when(owner(q) != r)
        def _():
            to_owner(q).wait_send()
    for off in range(1, reps):
        swap_reps(off).wait_send()

    @pl.loop(0, kb)
    def _(k):
        for off in range(1, n):
            shuffle(k, off).wait_send()
        for c in range(n):
            if c > 0:
                @pl.when((z <= c) & (z > 0))
                def _():
                    to_left(k, c).wait_send()
            if c < n - 1:
                @pl.when((z >= c) & (z < n - 1))
                def _():
                    to_right(k, c).wait_send()


def ladder_blocks(staged, integrals, n, reps):
    kb, rows, width = staged.shape[1:]
    slab_rows = integrals.shape[1]
    per_rep = -(-(n * (n + 1) // 2) // reps)
    slots = -(-per_rep // n)
    bf16, dma = jnp.bfloat16, pltpu.SemaphoreType.DMA
    return pl.pallas_call(
        functools.partial(kernel, n, reps),
        out_shape=jax.ShapeDtypeStruct((n, rows, slab_rows), bf16),
        in_specs=[pl.BlockSpec(memory_space=pltpu.VMEM), pl.BlockSpec(memory_space=pl.ANY)],
        out_specs=pl.BlockSpec(memory_space=pl.ANY),
        scratch_shapes=[
            pltpu.VMEM((kb, n, n, rows, width), bf16),
            pltpu.VMEM((reps * per_rep, rows, width), bf16),
            pltpu.VMEM((kb, slab_rows, width), bf16),
            pltpu.VMEM((reps * per_rep * rows, slab_rows), jnp.float32),
            pltpu.VMEM((reps, per_rep, rows, slab_rows), bf16),
            pltpu.VMEM((max(reps - 1, 1), per_rep, rows, slab_rows), bf16),
            pltpu.VMEM((per_rep, rows, slab_rows), bf16),
            pltpu.VMEM((slots, n, rows, slab_rows), bf16),
            pltpu.VMEM((slots, rows, slab_rows), bf16),
            dma((kb,)),
            dma((kb, n - 1)),
            dma((kb, n - 1)),
            dma((kb, n)),
            dma((kb, n)),
            dma((kb, n)),
            dma((max(reps - 1, 1),)),
            dma((max(reps - 1, 1),)),
            dma((per_rep,)),
            dma((slots, n)),
            dma((slots, reps, 2)),
            dma((n,)),
        ],
        compiler_params=pltpu.CompilerParams(
            collective_id=0, has_side_effects=True, vmem_limit_bytes=56 * 1024 * 1024),
        name="ladder_blocks",
    )(staged, integrals)


def shards(n, reps, amplitudes, integrals, occ_offsets, slab):
    block, _, kb, pairs = amplitudes.shape
    r, z = lax.axis_index("row"), lax.axis_index("col")
    natural = jnp.transpose(amplitudes.reshape(block, block, kb, n, pairs // n), (3, 2, 0, 1, 4))
    swapped = jnp.swapaxes(natural, 2, 3)
    mixed = (natural.astype(jnp.float32) - swapped.astype(jnp.float32)).astype(natural.dtype)
    staged = jnp.where(r < z, natural, jnp.where(r > z, swapped, mixed))
    staged = staged.reshape(n, kb, block * block, pairs // n)
    blocks = ladder_blocks(staged, jnp.transpose(integrals, (1, 0, 2)), n, reps)
    slab_rows = integrals.shape[0]
    found = jnp.transpose(blocks.reshape(n, block, block, slab_rows), (1, 2, 0, 3))
    found = found.reshape(block, block, n * slab_rows)
    found = jnp.where(r <= z, found, -jnp.swapaxes(found, 0, 1))
    row_orbitals = r * block + jnp.arange(block, dtype=jnp.int32)
    col_orbitals = z * block + jnp.arange(block, dtype=jnp.int32)
    target = jnp.bitwise_xor(slab[0], slab[1])
    row_labels = irrep_labels(row_orbitals, occ_offsets)
    col_labels = irrep_labels(col_orbitals, occ_offsets)
    allowed = jnp.bitwise_xor(row_labels[:, None], col_labels[None, :]) == target
    return jnp.where(allowed[:, :, None], found, jnp.bfloat16(0.0))


def solution(mesh):
    placed = (P("row", "col", "rep", None), P("col", "rep", "row"), P(), P())
    n, reps = mesh.shape["row"], mesh.shape["rep"]
    assert mesh.shape["col"] == n
    return jax.shard_map(
        functools.partial(shards, n, reps), mesh=mesh, in_specs=placed,
        out_specs=P("row", "col", None), check_vma=False
    )
```

```python
import functools

import jax
import jax.numpy as jnp
from jax import lax
from jax.experimental import pallas as pl
from jax.experimental.pallas import tpu as pltpu
from jax.sharding import PartitionSpec as P

MESH = pl.DeviceIdType.MESH


def irrep_labels(orbitals, occ_offsets):
    bound = jnp.arange(occ_offsets.shape[0], dtype=jnp.int32)
    inner = (bound >= 1) & (bound < occ_offsets.shape[0] - 1)
    return jnp.sum(((orbitals[:, None] >= occ_offsets[None, :]) & inner[None, :]).astype(jnp.int32), axis=1)


def pair_start(first, n):
    return first * (n - 1) - first * (first - 1) // 2


def swap_rows(block, size):
    return jnp.concatenate(
        [block[i * size + j : i * size + j + 1] for j in range(size) for i in range(size)], axis=0)


def pack_rows(block, size):
    above = [block[i * size + i + 1 : (i + 1) * size] for i in range(size - 1)]
    rest = size * size // 2 - size * (size - 1) // 2
    return jnp.concatenate(above + [jnp.zeros_like(block[:rest])], axis=0)


def unpack_rows(packed, size):
    rows, at = {}, 0
    for i in range(size):
        for j in range(i + 1, size):
            rows[i, j], rows[j, i] = packed[at : at + 1], -packed[at : at + 1]
            at += 1
        rows[i, i] = jnp.zeros_like(packed[:1])
    return jnp.concatenate([rows[i, j] for i in range(size) for j in range(size)], axis=0)


def kernel(n, reps, size, s_ref, v_hbm, out_ref, x, g, dd, v, acc, pb, rrecv, qb, rowrecv, res,
           lv, a_send, a_recv, l_send, r_send, x_recv, gl_send, gr_send, g_recv, p_send, p_recv, q_send, q_recv,
           o_send, o_recv):
    kb = s_ref.shape[1]
    per_rep = pb.shape[1]
    slots = res.shape[0]
    off_pairs = n * (n - 1) // 2
    numbers = off_pairs + -(-n // 2)
    half = s_ref.shape[2] // 2
    width = s_ref.shape[3]
    half_width = min(-(-width // 256) * 128, width)
    r, z, p = lax.axis_index("row"), lax.axis_index("col"), lax.axis_index("rep")

    def remote(src, dst, send, recv, **where):
        target = {"row": r, "col": z, "rep": p, **where}
        return pltpu.make_async_remote_copy(
            src_ref=src, dst_ref=dst, send_sem=send, recv_sem=recv,
            device_id=(target["row"], target["col"], target["rep"]), device_id_type=MESH)

    for k in range(kb):
        pltpu.make_async_copy(v_hbm.at[k], v.at[k], lv.at[k]).start()

    barrier = pltpu.get_barrier_semaphore()
    devices = n * n * reps
    me = (r * n + z) * reps + p

    @pl.loop(1, devices)
    def _(off):
        other = lax.rem(me + off, devices)
        pl.semaphore_signal(
            barrier, inc=1,
            device_id=(other // (n * reps), lax.rem(other // reps, n), lax.rem(other, reps)),
            device_id_type=MESH)

    pl.semaphore_wait(barrier, devices - 1)

    def shuffle(k, off):
        dest = lax.rem(r + off, n)
        return remote(s_ref.at[dest, k], x.at[k, z, r], a_send.at[k, off - 1],
                      a_recv.at[k, off - 1], row=dest)

    def shuffled(k, off):
        source = lax.rem(r + n - off, n)
        return remote(s_ref.at[source, k], x.at[k, z, source], a_send.at[k, off - 1],
                      a_recv.at[k, off - 1], row=source)

    for k in range(kb):
        for off in range(1, n):
            shuffle(k, off).start()
        x[k, z, r] = s_ref[r, k]
    acc[...] = jnp.zeros_like(acc)
    if reps * per_rep != numbers:
        dd[...] = jnp.zeros_like(dd)

    left, right = lax.max(z - 1, 0), lax.min(z + 1, n - 1)

    def to_left(k, c):
        part = x.at[k, c, pl.ds(0, c)]
        return remote(part, part, l_send.at[k, c], x_recv.at[k, c], col=left)

    def to_right(k, c):
        part = x.at[k, c, pl.ds(c + 1, n - 1 - c)]
        return remote(part, part, r_send.at[k, c], x_recv.at[k, c], col=right)

    def diagonal(m, c):
        return g.at[c, m] if 2 * m + 1 < kb else g.at[c, m, :, pl.ds(0, half_width)]

    def g_left(m, c):
        return remote(diagonal(m, c), diagonal(m, c), gl_send.at[m, c], g_recv.at[m, c], col=left)

    def g_right(m, c):
        return remote(diagonal(m, c), diagonal(m, c), gr_send.at[m, c], g_recv.at[m, c], col=right)

    def pack(m):
        first = pack_rows(x[2 * m, z, z].astype(jnp.float32), size)
        if 2 * m + 1 < kb:
            second = pack_rows(x[2 * m + 1, z, z].astype(jnp.float32), size)
            g[z, m] = jnp.concatenate([first, second], axis=0).astype(g.dtype)
        else:
            tail = first[:, half_width:]
            fill = jnp.zeros((half, 2 * half_width - width), jnp.float32)
            tail = jnp.concatenate([tail, fill], axis=1)
            g[z, m, :, pl.ds(0, half_width)] = jnp.concatenate(
                [first[:, :half_width], tail], axis=0).astype(g.dtype)

    def unpacked(k, c):
        m = k // 2
        if 2 * m + 1 < kb:
            both = g[c, m].astype(jnp.float32)
            return both[:half] if k % 2 == 0 else both[half:]
        both = g[c, m, :, pl.ds(0, half_width)].astype(jnp.float32)
        return jnp.concatenate([both[:half], both[half:, : width - half_width]], axis=1)

    for k in range(kb):
        for off in range(1, n):
            shuffled(k, off).wait_recv()
        for c in range(n):
            @pl.when(z == c)
            def _():
                if c > 0:
                    to_left(k, c).start()
                if c < n - 1:
                    to_right(k, c).start()
        if k % 2 == 1 or k == kb - 1:
            pack(k // 2)
            for c in range(n):
                @pl.when(z == c)
                def _():
                    if c > 0:
                        g_left(k // 2, c).start()
                    if c < n - 1:
                        g_right(k // 2, c).start()

    def slot_of(number):
        return number % reps * per_rep + number // reps

    def assemble(k, first, second):
        slot = slot_of(pair_start(first, n) + second - first - 1)

        @pl.when(z <= first)
        def _():
            dd[slot] = x[k, second, first]

        @pl.when(z >= second)
        def _():
            dd[slot] = x[k, first, second]

        if second - first > 1:
            @pl.when((z > first) & (z < second))
            def _():
                dd[slot] = (x[k, second, first].astype(jnp.float32)
                            - x[k, first, second].astype(jnp.float32)).astype(dd.dtype)

    def arrivals(k, d):
        for c in range(n):
            if c >= d:
                @pl.when(z == c - d)
                def _():
                    to_left(k, c).wait_recv()
                    x[k, c, c - d] = (x[k, c, c - d].astype(jnp.float32)
                                      - x[k, c - d, c].astype(jnp.float32)).astype(x.dtype)
                    if c > d:
                        to_left(k, c).start()
                    if k % 2 == 0:
                        g_left(k // 2, c).wait_recv()
                        if c > d:
                            g_left(k // 2, c).start()
            if c + d < n:
                @pl.when(z == c + d)
                def _():
                    to_right(k, c).wait_recv()
                    x[k, c, c + d] = (x[k, c + d, c].astype(jnp.float32)
                                      - x[k, c, c + d].astype(jnp.float32)).astype(x.dtype)
                    if c + d < n - 1:
                        to_right(k, c).start()
                    if k % 2 == 0:
                        g_right(k // 2, c).wait_recv()
                        if c + d < n - 1:
                            g_right(k // 2, c).start()

    for d in range(1, n):
        for k in range(kb):
            arrivals(k, d)
            if d == n - 1:
                for first in range(n):
                    for second in range(first + 1, n):
                        assemble(k, first, second)
                for c in range(0, n, 2):
                    one = unpacked(k, c)
                    two = unpacked(k, c + 1) if c + 1 < n else jnp.zeros_like(one)
                    dd[slot_of(off_pairs + c // 2)] = jnp.concatenate(
                        [one, two], axis=0).astype(dd.dtype)
                pltpu.make_async_copy(v_hbm.at[k], v.at[k], lv.at[k]).wait()
                acc[...] += lax.dot_general(
                    dd[...].reshape(acc.shape[0], dd.shape[2]), v[k],
                    (((1,), (1,)), ((), ())), preferred_element_type=jnp.float32)

    pb[...] = acc[...].reshape(pb.shape).astype(pb.dtype)

    def swap_reps(off):
        other = lax.rem(p + off, reps)
        return remote(pb.at[other], rrecv.at[off - 1], p_send.at[off - 1], p_recv.at[off - 1],
                      rep=other)

    for off in range(1, reps):
        swap_reps(off).start()
    for off in range(1, reps):
        swap_reps(off).wait_recv()

    flip = lax.rem(p, 2)

    def owner(q):
        return lax.rem(q, n) * (1 - 2 * flip) + (n - 1) * flip

    def to_owner(q):
        return remote(qb.at[q], rowrecv.at[q // n, r], q_send.at[q],
                      q_recv.at[q // n, r], row=owner(q))

    for q in range(per_rep):
        total = pb[p, q].astype(jnp.float32)
        for off in range(1, reps):
            total += rrecv[off - 1, q].astype(jnp.float32)
        qb[q] = total.astype(qb.dtype)

        @pl.when(owner(q) != r)
        def _():
            to_owner(q).start()

    mine = r * (1 - 2 * flip) + (n - 1) * flip

    def number_of(s):
        return (s * n + mine) * reps + p

    def deliver(s, do):
        number = number_of(s)
        first = 0
        for t in range(1, n - 1):
            first = first + (number >= pair_start(t, n)).astype(jnp.int32)
        second = number - pair_start(first, n) + first + 1
        even = 2 * (number - off_pairs)
        apart = number < off_pairs
        first, other = jnp.where(apart, first, even), jnp.where(apart, first, even + 1)
        second, swapped = jnp.where(apart, second, even), jnp.where(apart, second, even + 1)
        for rep in range(reps):
            for t, (row, col) in enumerate(((first, second), (swapped, other))):
                local = (row == r) & (col == z) & (p == rep)
                wanted = (row < n) & (col < n)

                @pl.when(wanted & local)
                def _():
                    if do == "start":
                        pltpu.make_async_copy(res.at[s, t], out_ref.at[z], o_recv.at[z]).start()

                @pl.when(wanted & jnp.logical_not(local))
                def _():
                    copy = remote(res.at[s, t], out_ref.at[z], o_send.at[s, rep, t],
                                  o_recv.at[z], row=row, col=col, rep=rep)
                    if do == "start":
                        copy.start()
                    else:
                        copy.wait_send()

    for s in range(slots):
        @pl.when((s * n + mine < per_rep) & (number_of(s) < numbers))
        def _():
            total = qb[s * n + mine].astype(jnp.float32)
            for off in range(1, n):
                source = lax.rem(r + off, n)
                remote(rowrecv.at[s, source], rowrecv.at[s, source], q_send.at[0],
                       q_recv.at[s, source], row=source).wait_recv()
                total += rowrecv[s, source].astype(jnp.float32)

            @pl.when(number_of(s) < off_pairs)
            def _():
                res[s, 0] = total.astype(res.dtype)
                res[s, 1] = (-swap_rows(total, size)).astype(res.dtype)

            @pl.when(number_of(s) >= off_pairs)
            def _():
                res[s, 0] = unpack_rows(total[:half], size).astype(res.dtype)
                res[s, 1] = unpack_rows(total[half:], size).astype(res.dtype)

            deliver(s, "start")

    for source in range(n):
        remote(out_ref.at[source], out_ref.at[source], o_send.at[0, 0, 0], o_recv.at[source],
               col=source).wait_recv()

    for s in range(slots):
        @pl.when((s * n + mine < per_rep) & (number_of(s) < numbers))
        def _():
            deliver(s, "wait")
    for q in range(per_rep):
        @pl.when(owner(q) != r)
        def _():
            to_owner(q).wait_send()
    for off in range(1, reps):
        swap_reps(off).wait_send()

    @pl.loop(0, kb)
    def _(k):
        for off in range(1, n):
            shuffle(k, off).wait_send()
        for c in range(n):
            if c > 0:
                @pl.when((z <= c) & (z > 0))
                def _():
                    to_left(k, c).wait_send()
            if c < n - 1:
                @pl.when((z >= c) & (z < n - 1))
                def _():
                    to_right(k, c).wait_send()

    for m in range(-(-kb // 2)):
        for c in range(n):
            if c > 0:
                @pl.when((z <= c) & (z > 0))
                def _():
                    g_left(m, c).wait_send()
            if c < n - 1:
                @pl.when((z >= c) & (z < n - 1))
                def _():
                    g_right(m, c).wait_send()


def ladder_blocks(staged, integrals, n, reps, size):
    kb, rows, width = staged.shape[1:]
    slab_rows = integrals.shape[1]
    numbers = n * (n - 1) // 2 + -(-n // 2)
    chunks = -(-kb // 2)
    per_rep = -(-numbers // reps)
    slots = -(-per_rep // n)
    bf16, dma = jnp.bfloat16, pltpu.SemaphoreType.DMA
    return pl.pallas_call(
        functools.partial(kernel, n, reps, size),
        out_shape=jax.ShapeDtypeStruct((n, rows, slab_rows), bf16),
        in_specs=[pl.BlockSpec(memory_space=pltpu.VMEM), pl.BlockSpec(memory_space=pl.ANY)],
        out_specs=pl.BlockSpec(memory_space=pl.ANY),
        scratch_shapes=[
            pltpu.VMEM((kb, n, n, rows, width), bf16),
            pltpu.VMEM((n, chunks, rows, width), bf16),
            pltpu.VMEM((reps * per_rep, rows, width), bf16),
            pltpu.VMEM((kb, slab_rows, width), bf16),
            pltpu.VMEM((reps * per_rep * rows, slab_rows), jnp.float32),
            pltpu.VMEM((reps, per_rep, rows, slab_rows), bf16),
            pltpu.VMEM((max(reps - 1, 1), per_rep, rows, slab_rows), bf16),
            pltpu.VMEM((per_rep, rows, slab_rows), bf16),
            pltpu.VMEM((slots, n, rows, slab_rows), bf16),
            pltpu.VMEM((slots, 2, rows, slab_rows), bf16),
            dma((kb,)),
            dma((kb, n - 1)),
            dma((kb, n - 1)),
            dma((kb, n)),
            dma((kb, n)),
            dma((kb, n)),
            dma((chunks, n)),
            dma((chunks, n)),
            dma((chunks, n)),
            dma((max(reps - 1, 1),)),
            dma((max(reps - 1, 1),)),
            dma((per_rep,)),
            dma((slots, n)),
            dma((slots, reps, 2)),
            dma((n,)),
        ],
        compiler_params=pltpu.CompilerParams(
            collective_id=0, has_side_effects=True, vmem_limit_bytes=56 * 1024 * 1024),
        name="ladder_blocks",
    )(staged, integrals)


def shards(n, reps, amplitudes, integrals, occ_offsets, slab):
    block, _, kb, pairs = amplitudes.shape
    r, z = lax.axis_index("row"), lax.axis_index("col")
    natural = jnp.transpose(amplitudes.reshape(block, block, kb, n, pairs // n), (3, 2, 0, 1, 4))
    swapped = jnp.swapaxes(natural, 2, 3)
    mixed = (natural.astype(jnp.float32) - swapped.astype(jnp.float32)).astype(natural.dtype)
    staged = jnp.where(r < z, natural, jnp.where(r > z, swapped, mixed))
    staged = staged.reshape(n, kb, block * block, pairs // n)
    blocks = ladder_blocks(staged, jnp.transpose(integrals, (1, 0, 2)), n, reps, block)
    slab_rows = integrals.shape[0]
    found = jnp.transpose(blocks.reshape(n, block, block, slab_rows), (1, 2, 0, 3))
    found = found.reshape(block, block, n * slab_rows)
    row_orbitals = r * block + jnp.arange(block, dtype=jnp.int32)
    col_orbitals = z * block + jnp.arange(block, dtype=jnp.int32)
    target = jnp.bitwise_xor(slab[0], slab[1])
    row_labels = irrep_labels(row_orbitals, occ_offsets)
    col_labels = irrep_labels(col_orbitals, occ_offsets)
    allowed = jnp.bitwise_xor(row_labels[:, None], col_labels[None, :]) == target
    return jnp.where(allowed[:, :, None], found, jnp.bfloat16(0.0))


def solution(mesh):
    placed = (P("row", "col", "rep", None), P("col", "rep", "row"), P(), P())
    n, reps = mesh.shape["row"], mesh.shape["rep"]
    assert mesh.shape["col"] == n
    return jax.shard_map(
        functools.partial(shards, n, reps), mesh=mesh, in_specs=placed,
        out_specs=P("row", "col", None), check_vma=False
    )
```

```python
import functools

import jax
import jax.numpy as jnp
from jax import lax
from jax.experimental import pallas as pl
from jax.experimental.pallas import tpu as pltpu
from jax.sharding import PartitionSpec as P

MESH = pl.DeviceIdType.MESH


def pair_start(first, n):
    return first * (n - 1) - first * (first - 1) // 2


def swap_rows(block, size):
    return jnp.concatenate(
        [block[i * size + j : i * size + j + 1] for j in range(size) for i in range(size)], axis=0)


def pack_rows(block, size):
    above = [block[i * size + i + 1 : (i + 1) * size] for i in range(size - 1)]
    rest = size * size // 2 - size * (size - 1) // 2
    return jnp.concatenate(above + [jnp.zeros_like(block[:rest])], axis=0)


def unpack_rows(packed, size):
    rows, at = {}, 0
    for i in range(size):
        for j in range(i + 1, size):
            rows[i, j], rows[j, i] = packed[at : at + 1], -packed[at : at + 1]
            at += 1
        rows[i, i] = jnp.zeros_like(packed[:1])
    return jnp.concatenate([rows[i, j] for i in range(size) for j in range(size)], axis=0)


def kernel(n, reps, size, a_ref, v_hbm, occ_ref, slab_ref, out_ref, s_ref, found, x, g, dd, v, acc, pb, rrecv, qb, rowrecv, res,
           lv, a_send, a_recv, l_send, r_send, x_recv, gl_send, gr_send, g_recv, p_send, p_recv, q_send, q_recv,
           o_send, o_recv):
    kb = s_ref.shape[1]
    f32 = jnp.float32
    per_rep = pb.shape[1]
    slots = res.shape[0]
    off_pairs = n * (n - 1) // 2
    numbers = off_pairs + -(-n // 2)
    half = s_ref.shape[2] // 2
    width = s_ref.shape[3]
    half_width = min(-(-width // 256) * 128, width)
    r, z, p = lax.axis_index("row"), lax.axis_index("col"), lax.axis_index("rep")

    def remote(src, dst, send, recv, **where):
        target = {"row": r, "col": z, "rep": p, **where}
        return pltpu.make_async_remote_copy(
            src_ref=src, dst_ref=dst, send_sem=send, recv_sem=recv,
            device_id=(target["row"], target["col"], target["rep"]), device_id_type=MESH)

    for k in range(kb):
        pltpu.make_async_copy(v_hbm.at[k], v.at[k], lv.at[k]).start()

    barrier = pltpu.get_barrier_semaphore()
    devices = n * n * reps
    me = (r * n + z) * reps + p

    @pl.loop(1, devices)
    def _(off):
        other = lax.rem(me + off, devices)
        pl.semaphore_signal(
            barrier, inc=1,
            device_id=(other // (n * reps), lax.rem(other // reps, n), lax.rem(other, reps)),
            device_id_type=MESH)

    def shuffle(k, off):
        dest = lax.rem(r + off, n)
        return remote(s_ref.at[dest, k], x.at[k, z, r], a_send.at[k, off - 1],
                      a_recv.at[k, off - 1], row=dest)

    def shuffled(k, off):
        source = lax.rem(r + n - off, n)
        return remote(s_ref.at[source, k], x.at[k, z, source], a_send.at[k, off - 1],
                      a_recv.at[k, off - 1], row=source)

    def stage(k):
        for dest in range(n):
            natural = jnp.concatenate(
                [a_ref[i, k, :, dest * width : (dest + 1) * width].astype(f32) for i in range(size)],
                axis=0)

            @pl.when(r < z)
            def _():
                s_ref[dest, k] = natural.astype(s_ref.dtype)

            @pl.when(r > z)
            def _():
                s_ref[dest, k] = swap_rows(natural, size).astype(s_ref.dtype)

            @pl.when(r == z)
            def _():
                s_ref[dest, k] = (natural - swap_rows(natural, size)).astype(s_ref.dtype)

    stage(0)
    acc[...] = jnp.zeros_like(acc)
    if reps * per_rep != numbers:
        dd[...] = jnp.zeros_like(dd)
    pl.semaphore_wait(barrier, devices - 1)
    for k in range(kb):
        for off in range(1, n):
            shuffle(k, off).start()
        x[k, z, r] = s_ref[r, k]
        if k + 1 < kb:
            stage(k + 1)

    left, right = lax.max(z - 1, 0), lax.min(z + 1, n - 1)

    def to_left(k, c):
        part = x.at[k, c, pl.ds(0, c)]
        return remote(part, part, l_send.at[k, c], x_recv.at[k, c], col=left)

    def to_right(k, c):
        part = x.at[k, c, pl.ds(c + 1, n - 1 - c)]
        return remote(part, part, r_send.at[k, c], x_recv.at[k, c], col=right)

    def diagonal(m, c):
        return g.at[c, m] if 2 * m + 1 < kb else g.at[c, m, :, pl.ds(0, half_width)]

    def g_left(m, c):
        return remote(diagonal(m, c), diagonal(m, c), gl_send.at[m, c], g_recv.at[m, c], col=left)

    def g_right(m, c):
        return remote(diagonal(m, c), diagonal(m, c), gr_send.at[m, c], g_recv.at[m, c], col=right)

    def pack(m):
        first = pack_rows(x[2 * m, z, z].astype(jnp.float32), size)
        if 2 * m + 1 < kb:
            second = pack_rows(x[2 * m + 1, z, z].astype(jnp.float32), size)
            g[z, m] = jnp.concatenate([first, second], axis=0).astype(g.dtype)
        else:
            tail = first[:, half_width:]
            fill = jnp.zeros((half, 2 * half_width - width), jnp.float32)
            tail = jnp.concatenate([tail, fill], axis=1)
            g[z, m, :, pl.ds(0, half_width)] = jnp.concatenate(
                [first[:, :half_width], tail], axis=0).astype(g.dtype)

    def unpacked(k, c):
        m = k // 2
        if 2 * m + 1 < kb:
            both = g[c, m].astype(jnp.float32)
            return both[:half] if k % 2 == 0 else both[half:]
        both = g[c, m, :, pl.ds(0, half_width)].astype(jnp.float32)
        return jnp.concatenate([both[:half], both[half:, : width - half_width]], axis=1)

    for k in range(kb):
        for off in range(1, n):
            shuffled(k, off).wait_recv()
        for c in range(n):
            @pl.when(z == c)
            def _():
                if c > 0:
                    to_left(k, c).start()
                if c < n - 1:
                    to_right(k, c).start()
        if k % 2 == 1 or k == kb - 1:
            pack(k // 2)
            for c in range(n):
                @pl.when(z == c)
                def _():
                    if c > 0:
                        g_left(k // 2, c).start()
                    if c < n - 1:
                        g_right(k // 2, c).start()

    def slot_of(number):
        return number % reps * per_rep + number // reps

    def assemble(k, first, second):
        slot = slot_of(pair_start(first, n) + second - first - 1)

        @pl.when(z <= first)
        def _():
            dd[slot] = x[k, second, first]

        @pl.when(z >= second)
        def _():
            dd[slot] = x[k, first, second]

        if second - first > 1:
            @pl.when((z > first) & (z < second))
            def _():
                dd[slot] = (x[k, second, first].astype(jnp.float32)
                            - x[k, first, second].astype(jnp.float32)).astype(dd.dtype)

    def arrivals(k, d):
        for c in range(n):
            if c >= d:
                @pl.when(z == c - d)
                def _():
                    to_left(k, c).wait_recv()
                    x[k, c, c - d] = (x[k, c, c - d].astype(jnp.float32)
                                      - x[k, c - d, c].astype(jnp.float32)).astype(x.dtype)
                    if c > d:
                        to_left(k, c).start()
                    if k % 2 == 0:
                        g_left(k // 2, c).wait_recv()
                        if c > d:
                            g_left(k // 2, c).start()
            if c + d < n:
                @pl.when(z == c + d)
                def _():
                    to_right(k, c).wait_recv()
                    x[k, c, c + d] = (x[k, c + d, c].astype(jnp.float32)
                                      - x[k, c, c + d].astype(jnp.float32)).astype(x.dtype)
                    if c + d < n - 1:
                        to_right(k, c).start()
                    if k % 2 == 0:
                        g_right(k // 2, c).wait_recv()
                        if c + d < n - 1:
                            g_right(k // 2, c).start()

    for d in range(1, n):
        for k in range(kb):
            arrivals(k, d)
            if d == n - 1:
                for first in range(n):
                    for second in range(first + 1, n):
                        assemble(k, first, second)
                for c in range(0, n, 2):
                    one = unpacked(k, c)
                    two = unpacked(k, c + 1) if c + 1 < n else jnp.zeros_like(one)
                    dd[slot_of(off_pairs + c // 2)] = jnp.concatenate(
                        [one, two], axis=0).astype(dd.dtype)
                pltpu.make_async_copy(v_hbm.at[k], v.at[k], lv.at[k]).wait()
                acc[...] += lax.dot_general(
                    v[k], dd[...].reshape(acc.shape[1], dd.shape[2]),
                    (((1,), (1,)), ((), ())), preferred_element_type=jnp.float32)

    pb[...] = acc[...].T.reshape(pb.shape).astype(pb.dtype)

    def swap_reps(off):
        other = lax.rem(p + off, reps)
        return remote(pb.at[other], rrecv.at[off - 1], p_send.at[off - 1], p_recv.at[off - 1],
                      rep=other)

    for off in range(1, reps):
        swap_reps(off).start()
    for off in range(1, reps):
        swap_reps(off).wait_recv()

    flip = lax.rem(p, 2)

    def owner(q):
        return lax.rem(q, n) * (1 - 2 * flip) + (n - 1) * flip

    def to_owner(q):
        return remote(qb.at[q], rowrecv.at[q // n, r], q_send.at[q],
                      q_recv.at[q // n, r], row=owner(q))

    for q in range(per_rep):
        total = pb[p, q].astype(jnp.float32)
        for off in range(1, reps):
            total += rrecv[off - 1, q].astype(jnp.float32)
        qb[q] = total.astype(qb.dtype)

        @pl.when(owner(q) != r)
        def _():
            to_owner(q).start()

    mine = r * (1 - 2 * flip) + (n - 1) * flip

    place = lax.broadcasted_iota(jnp.int32, (size * size, 128), 0)
    place_i = sum((place >= t * size).astype(jnp.int32) for t in range(1, size))
    place_j = place - size * place_i
    target = jnp.bitwise_xor(slab_ref[0], slab_ref[1])

    def labels(orbitals):
        return sum((orbitals >= occ_ref[t]).astype(jnp.int32)
                   for t in range(1, occ_ref.shape[0] - 1))

    def masked(block, first, second):
        mixed = jnp.bitwise_xor(labels(first * size + place_i), labels(second * size + place_j))
        allowed = (mixed == target).astype(f32)[:, :1]
        return jnp.where(jnp.broadcast_to(allowed, block.shape) > 0, block, jnp.zeros_like(block))

    def number_of(s):
        return (s * n + mine) * reps + p

    def blocks_of(s):
        number = number_of(s)
        first = 0
        for t in range(1, n - 1):
            first = first + (number >= pair_start(t, n)).astype(jnp.int32)
        second = number - pair_start(first, n) + first + 1
        even = 2 * (number - off_pairs)
        apart = number < off_pairs
        first, other = jnp.where(apart, first, even), jnp.where(apart, first, even + 1)
        second, swapped = jnp.where(apart, second, even), jnp.where(apart, second, even + 1)
        return first, second, other, swapped

    def deliver(s, do):
        first, second, other, swapped = blocks_of(s)
        for rep in range(reps):
            for t, (row, col) in enumerate(((first, second), (swapped, other))):
                local = (row == r) & (col == z) & (p == rep)
                wanted = (row < n) & (col < n)

                @pl.when(wanted & local)
                def _():
                    if do == "start":
                        pltpu.make_async_copy(res.at[s, t], found.at[z], o_recv.at[z]).start()

                @pl.when(wanted & jnp.logical_not(local))
                def _():
                    copy = remote(res.at[s, t], found.at[z], o_send.at[s, rep, t],
                                  o_recv.at[z], row=row, col=col, rep=rep)
                    if do == "start":
                        copy.start()
                    else:
                        copy.wait_send()

    for s in range(slots):
        @pl.when((s * n + mine < per_rep) & (number_of(s) < numbers))
        def _():
            total = qb[s * n + mine].astype(jnp.float32)
            for off in range(1, n):
                source = lax.rem(r + off, n)
                remote(rowrecv.at[s, source], rowrecv.at[s, source], q_send.at[0],
                       q_recv.at[s, source], row=source).wait_recv()
                total += rowrecv[s, source].astype(jnp.float32)

            first, second, other, _swapped = blocks_of(s)

            @pl.when(number_of(s) < off_pairs)
            def _():
                kept = masked(total, first, second)
                res[s, 0] = kept.astype(res.dtype)
                res[s, 1] = (-swap_rows(kept, size)).astype(res.dtype)

            @pl.when(number_of(s) >= off_pairs)
            def _():
                res[s, 0] = masked(unpack_rows(total[:half], size), first, first).astype(res.dtype)
                res[s, 1] = masked(unpack_rows(total[half:], size), other, other).astype(res.dtype)

            deliver(s, "start")

    for source in range(n):
        remote(found.at[source], found.at[source], o_send.at[0, 0, 0], o_recv.at[source],
               col=source).wait_recv()

    whole = jnp.concatenate([found[source].astype(f32) for source in range(n)], axis=1)
    for i in range(size):
        out_ref[i] = whole[i * size : (i + 1) * size].astype(out_ref.dtype)

    for s in range(slots):
        @pl.when((s * n + mine < per_rep) & (number_of(s) < numbers))
        def _():
            deliver(s, "wait")
    for q in range(per_rep):
        @pl.when(owner(q) != r)
        def _():
            to_owner(q).wait_send()
    for off in range(1, reps):
        swap_reps(off).wait_send()

    @pl.loop(0, kb)
    def _(k):
        for off in range(1, n):
            shuffle(k, off).wait_send()
        for c in range(n):
            if c > 0:
                @pl.when((z <= c) & (z > 0))
                def _():
                    to_left(k, c).wait_send()
            if c < n - 1:
                @pl.when((z >= c) & (z < n - 1))
                def _():
                    to_right(k, c).wait_send()

    for m in range(-(-kb // 2)):
        for c in range(n):
            if c > 0:
                @pl.when((z <= c) & (z > 0))
                def _():
                    g_left(m, c).wait_send()
            if c < n - 1:
                @pl.when((z >= c) & (z < n - 1))
                def _():
                    g_right(m, c).wait_send()


def ladder_blocks(amplitudes, integrals, occ_offsets, slab, n, reps):
    size, kb, _, pairs = amplitudes.shape
    rows, width = size * size, pairs // n
    slab_rows = integrals.shape[1]
    numbers = n * (n - 1) // 2 + -(-n // 2)
    chunks = -(-kb // 2)
    per_rep = -(-numbers // reps)
    slots = -(-per_rep // n)
    bf16, dma = jnp.bfloat16, pltpu.SemaphoreType.DMA
    return pl.pallas_call(
        functools.partial(kernel, n, reps, size),
        out_shape=jax.ShapeDtypeStruct((size, size, n * slab_rows), bf16),
        in_specs=[
            pl.BlockSpec(memory_space=pltpu.VMEM),
            pl.BlockSpec(memory_space=pl.ANY),
            pl.BlockSpec(memory_space=pltpu.SMEM),
            pl.BlockSpec(memory_space=pltpu.SMEM),
        ],
        out_specs=pl.BlockSpec(memory_space=pltpu.VMEM),
        scratch_shapes=[
            pltpu.VMEM((n, kb, rows, width), bf16),
            pltpu.VMEM((n, rows, slab_rows), bf16),
            pltpu.VMEM((kb, n, n, rows, width), bf16),
            pltpu.VMEM((n, chunks, rows, width), bf16),
            pltpu.VMEM((reps * per_rep, rows, width), bf16),
            pltpu.VMEM((kb, slab_rows, width), bf16),
            pltpu.VMEM((slab_rows, reps * per_rep * rows), jnp.float32),
            pltpu.VMEM((reps, per_rep, rows, slab_rows), bf16),
            pltpu.VMEM((max(reps - 1, 1), per_rep, rows, slab_rows), bf16),
            pltpu.VMEM((per_rep, rows, slab_rows), bf16),
            pltpu.VMEM((slots, n, rows, slab_rows), bf16),
            pltpu.VMEM((slots, 2, rows, slab_rows), bf16),
            dma((kb,)),
            dma((kb, n - 1)),
            dma((kb, n - 1)),
            dma((kb, n)),
            dma((kb, n)),
            dma((kb, n)),
            dma((chunks, n)),
            dma((chunks, n)),
            dma((chunks, n)),
            dma((max(reps - 1, 1),)),
            dma((max(reps - 1, 1),)),
            dma((per_rep,)),
            dma((slots, n)),
            dma((slots, reps, 2)),
            dma((n,)),
        ],
        compiler_params=pltpu.CompilerParams(
            collective_id=0, has_side_effects=True, vmem_limit_bytes=56 * 1024 * 1024),
        name="ladder_blocks",
    )(amplitudes, integrals, occ_offsets, slab)


def shards(n, reps, amplitudes, integrals, occ_offsets, slab):
    return ladder_blocks(
        jnp.transpose(amplitudes, (0, 2, 1, 3)), jnp.transpose(integrals, (1, 0, 2)),
        occ_offsets, slab, n, reps)


def solution(mesh):
    placed = (P("row", "col", "rep", None), P("col", "rep", "row"), P(), P())
    n, reps = mesh.shape["row"], mesh.shape["rep"]
    assert mesh.shape["col"] == n
    return jax.shard_map(
        functools.partial(shards, n, reps), mesh=mesh, in_specs=placed,
        out_specs=P("row", "col", None), check_vma=False
    )
```

```python
import functools

import jax
import jax.numpy as jnp
from jax import lax
from jax.experimental import pallas as pl
from jax.experimental.pallas import tpu as pltpu
from jax.sharding import PartitionSpec as P

MESH = pl.DeviceIdType.MESH


def pair_start(first, n):
    return first * (n - 1) - first * (first - 1) // 2


def swap_rows(block, size):
    return jnp.concatenate(
        [block[i * size + j : i * size + j + 1] for j in range(size) for i in range(size)], axis=0)


def pack_rows(block, size):
    above = [block[i * size + i + 1 : (i + 1) * size] for i in range(size - 1)]
    rest = size * size // 2 - size * (size - 1) // 2
    return jnp.concatenate(above + [jnp.zeros_like(block[:rest])], axis=0)


def unpack_rows(packed, size):
    rows, at = {}, 0
    for i in range(size):
        for j in range(i + 1, size):
            rows[i, j], rows[j, i] = packed[at : at + 1], -packed[at : at + 1]
            at += 1
        rows[i, i] = jnp.zeros_like(packed[:1])
    return jnp.concatenate([rows[i, j] for i in range(size) for j in range(size)], axis=0)


def kernel(n, reps, size, a_hbm, v_hbm, occ_ref, slab_ref, out_ref, a_ref, s_ref, found, x, g, dd, v, acc, pb, rrecv, qb, rowrecv, res,
           la, lv, a_send, a_recv, l_send, r_send, x_recv, gl_send, gr_send, g_recv, p_send, p_recv, q_send, q_recv,
           o_send, o_recv):
    kb = s_ref.shape[1]
    f32 = jnp.float32
    per_rep = pb.shape[1]
    slots = res.shape[0]
    off_pairs = n * (n - 1) // 2
    numbers = off_pairs + -(-n // 2)
    half = s_ref.shape[2] // 2
    width = s_ref.shape[3]
    half_width = min(-(-width // 256) * 128, width)
    r, z, p = lax.axis_index("row"), lax.axis_index("col"), lax.axis_index("rep")

    def remote(src, dst, send, recv, **where):
        target = {"row": r, "col": z, "rep": p, **where}
        return pltpu.make_async_remote_copy(
            src_ref=src, dst_ref=dst, send_sem=send, recv_sem=recv,
            device_id=(target["row"], target["col"], target["rep"]), device_id_type=MESH)

    fetch = pltpu.make_async_copy(a_hbm, a_ref, la)
    fetch.start()
    for k in range(kb):
        pltpu.make_async_copy(v_hbm.at[k], v.at[k], lv.at[k]).start()

    barrier = pltpu.get_barrier_semaphore()
    devices = n * n * reps
    me = (r * n + z) * reps + p

    @pl.loop(1, devices)
    def _(off):
        other = lax.rem(me + off, devices)
        pl.semaphore_signal(
            barrier, inc=1,
            device_id=(other // (n * reps), lax.rem(other // reps, n), lax.rem(other, reps)),
            device_id_type=MESH)

    def shuffle(k, off):
        dest = lax.rem(r + off, n)
        return remote(s_ref.at[dest, k], x.at[k, z, r], a_send.at[k, off - 1],
                      a_recv.at[k, off - 1], row=dest)

    def shuffled(k, off):
        source = lax.rem(r + n - off, n)
        return remote(s_ref.at[source, k], x.at[k, z, source], a_send.at[k, off - 1],
                      a_recv.at[k, off - 1], row=source)

    def stage(k):
        for dest in range(n):
            natural = jnp.concatenate(
                [a_ref[i, k, :, dest * width : (dest + 1) * width].astype(f32) for i in range(size)],
                axis=0)

            @pl.when(r < z)
            def _():
                s_ref[dest, k] = natural.astype(s_ref.dtype)

            @pl.when(r > z)
            def _():
                s_ref[dest, k] = swap_rows(natural, size).astype(s_ref.dtype)

            @pl.when(r == z)
            def _():
                s_ref[dest, k] = (natural - swap_rows(natural, size)).astype(s_ref.dtype)

    acc[...] = jnp.zeros_like(acc)
    fetch.wait()
    stage(0)
    if reps * per_rep != numbers:
        dd[...] = jnp.zeros_like(dd)
    pl.semaphore_wait(barrier, devices - 1)
    def send_shuffle(k):
        for off in range(1, n):
            shuffle(k, off).start()
        x[k, z, r] = s_ref[r, k]

    send_shuffle(0)
    if kb > 1:
        stage(1)
        send_shuffle(1)

    left, right = lax.max(z - 1, 0), lax.min(z + 1, n - 1)

    def to_left(k, c):
        part = x.at[k, c, pl.ds(0, c)]
        return remote(part, part, l_send.at[k, c], x_recv.at[k, c], col=left)

    def to_right(k, c):
        part = x.at[k, c, pl.ds(c + 1, n - 1 - c)]
        return remote(part, part, r_send.at[k, c], x_recv.at[k, c], col=right)

    def diagonal(m, c):
        return g.at[c, m] if 2 * m + 1 < kb else g.at[c, m, :, pl.ds(0, half_width)]

    def g_left(m, c):
        return remote(diagonal(m, c), diagonal(m, c), gl_send.at[m, c], g_recv.at[m, c], col=left)

    def g_right(m, c):
        return remote(diagonal(m, c), diagonal(m, c), gr_send.at[m, c], g_recv.at[m, c], col=right)

    def pack(m):
        first = pack_rows(x[2 * m, z, z].astype(jnp.float32), size)
        if 2 * m + 1 < kb:
            second = pack_rows(x[2 * m + 1, z, z].astype(jnp.float32), size)
            g[z, m] = jnp.concatenate([first, second], axis=0).astype(g.dtype)
        else:
            tail = first[:, half_width:]
            fill = jnp.zeros((half, 2 * half_width - width), jnp.float32)
            tail = jnp.concatenate([tail, fill], axis=1)
            g[z, m, :, pl.ds(0, half_width)] = jnp.concatenate(
                [first[:, :half_width], tail], axis=0).astype(g.dtype)

    def unpacked(k, c):
        m = k // 2
        if 2 * m + 1 < kb:
            both = g[c, m].astype(jnp.float32)
            return both[:half] if k % 2 == 0 else both[half:]
        both = g[c, m, :, pl.ds(0, half_width)].astype(jnp.float32)
        return jnp.concatenate([both[:half], both[half:, : width - half_width]], axis=1)

    for k in range(kb):
        for off in range(1, n):
            shuffled(k, off).wait_recv()
        for c in range(n):
            @pl.when(z == c)
            def _():
                if c > 0:
                    to_left(k, c).start()
                if c < n - 1:
                    to_right(k, c).start()
        if k + 2 < kb:
            stage(k + 2)
            send_shuffle(k + 2)
        if k % 2 == 1 or k == kb - 1:
            pack(k // 2)
            for c in range(n):
                @pl.when(z == c)
                def _():
                    if c > 0:
                        g_left(k // 2, c).start()
                    if c < n - 1:
                        g_right(k // 2, c).start()

    def slot_of(number):
        return number % reps * per_rep + number // reps

    def assemble(k, first, second):
        slot = slot_of(pair_start(first, n) + second - first - 1)

        @pl.when(z <= first)
        def _():
            dd[slot] = x[k, second, first]

        @pl.when(z >= second)
        def _():
            dd[slot] = x[k, first, second]

        @pl.when((z > first) & (z < second))
        def _():
            dd[slot] = (x[k, second, first].astype(f32)
                        - x[k, first, second].astype(f32)).astype(dd.dtype)

    def arrivals(k, d):
        for c in range(n):
            if c >= d:
                @pl.when(z == c - d)
                def _():
                    to_left(k, c).wait_recv()
                    x[k, c, c - d] = (x[k, c, c - d].astype(f32)
                                      - x[k, c - d, c].astype(f32)).astype(x.dtype)
                    if c > d:
                        to_left(k, c).start()
                    for m in range(-(-kb // 2)):
                        @pl.when(k == 2 * m)
                        def _():
                            g_left(m, c).wait_recv()
                            if c > d:
                                g_left(m, c).start()
            if c + d < n:
                @pl.when(z == c + d)
                def _():
                    to_right(k, c).wait_recv()
                    x[k, c, c + d] = (x[k, c + d, c].astype(f32)
                                      - x[k, c, c + d].astype(f32)).astype(x.dtype)
                    if c + d < n - 1:
                        to_right(k, c).start()
                    for m in range(-(-kb // 2)):
                        @pl.when(k == 2 * m)
                        def _():
                            g_right(m, c).wait_recv()
                            if c + d < n - 1:
                                g_right(m, c).start()

    def multiply(k):
        @pl.loop(0, n - 1)
        def _(first):
            @pl.loop(first + 1, n)
            def _(second):
                assemble(k, first, second)

        for now in range(kb):
            @pl.when(k == now)
            def _():
                for c in range(0, n, 2):
                    one = unpacked(now, c)
                    two = unpacked(now, c + 1) if c + 1 < n else jnp.zeros_like(one)
                    dd[slot_of(off_pairs + c // 2)] = jnp.concatenate(
                        [one, two], axis=0).astype(dd.dtype)

        pltpu.make_async_copy(v_hbm.at[k], v.at[k], lv.at[k]).wait()
        acc[...] += lax.dot_general(
            v[k], dd[...].reshape(acc.shape[1], dd.shape[2]),
            (((1,), (1,)), ((), ())), preferred_element_type=f32)

    last = lax.max(z, n - 1 - z)
    for d in range(1, n):
        @pl.loop(0, kb)
        def _(k):
            arrivals(k, d)
            if 2 * d >= n - 1:
                @pl.when(d == last)
                def _():
                    multiply(k)

    pb[...] = acc[...].T.reshape(pb.shape).astype(pb.dtype)

    def swap_reps(off):
        other = lax.rem(p + off, reps)
        return remote(pb.at[other], rrecv.at[off - 1], p_send.at[off - 1], p_recv.at[off - 1],
                      rep=other)

    for off in range(1, reps):
        swap_reps(off).start()
    for off in range(1, reps):
        swap_reps(off).wait_recv()

    flip = lax.rem(p, 2)

    def owner(q):
        return lax.rem(q, n) * (1 - 2 * flip) + (n - 1) * flip

    def to_owner(q):
        return remote(qb.at[q], rowrecv.at[q // n, r], q_send.at[q],
                      q_recv.at[q // n, r], row=owner(q))

    for q in range(per_rep):
        total = pb[p, q].astype(jnp.float32)
        for off in range(1, reps):
            total += rrecv[off - 1, q].astype(jnp.float32)
        qb[q] = total.astype(qb.dtype)

        @pl.when(owner(q) != r)
        def _():
            to_owner(q).start()

    mine = r * (1 - 2 * flip) + (n - 1) * flip

    place = lax.broadcasted_iota(jnp.int32, (size * size, 128), 0)
    place_i = sum((place >= t * size).astype(jnp.int32) for t in range(1, size))
    place_j = place - size * place_i
    target = jnp.bitwise_xor(slab_ref[0], slab_ref[1])

    def labels(orbitals):
        return sum((orbitals >= occ_ref[t]).astype(jnp.int32)
                   for t in range(1, occ_ref.shape[0] - 1))

    def masked(block, first, second):
        mixed = jnp.bitwise_xor(labels(first * size + place_i), labels(second * size + place_j))
        allowed = (mixed == target).astype(f32)[:, :1]
        return jnp.where(jnp.broadcast_to(allowed, block.shape) > 0, block, jnp.zeros_like(block))

    def number_of(s):
        return (s * n + mine) * reps + p

    def blocks_of(s):
        number = number_of(s)
        first = 0
        for t in range(1, n - 1):
            first = first + (number >= pair_start(t, n)).astype(jnp.int32)
        second = number - pair_start(first, n) + first + 1
        even = 2 * (number - off_pairs)
        apart = number < off_pairs
        first, other = jnp.where(apart, first, even), jnp.where(apart, first, even + 1)
        second, swapped = jnp.where(apart, second, even), jnp.where(apart, second, even + 1)
        return first, second, other, swapped

    def deliver(s, do):
        first, second, other, swapped = blocks_of(s)
        for rep in range(reps):
            for t, (row, col) in enumerate(((first, second), (swapped, other))):
                local = (row == r) & (col == z) & (p == rep)
                wanted = (row < n) & (col < n)

                @pl.when(wanted & local)
                def _():
                    if do == "start":
                        pltpu.make_async_copy(res.at[s, t], found.at[z], o_recv.at[z]).start()

                @pl.when(wanted & jnp.logical_not(local))
                def _():
                    copy = remote(res.at[s, t], found.at[z], o_send.at[s, rep, t],
                                  o_recv.at[z], row=row, col=col, rep=rep)
                    if do == "start":
                        copy.start()
                    else:
                        copy.wait_send()

    for s in range(slots):
        @pl.when((s * n + mine < per_rep) & (number_of(s) < numbers))
        def _():
            total = qb[s * n + mine].astype(jnp.float32)
            for off in range(1, n):
                source = lax.rem(r + off, n)
                remote(rowrecv.at[s, source], rowrecv.at[s, source], q_send.at[0],
                       q_recv.at[s, source], row=source).wait_recv()
                total += rowrecv[s, source].astype(jnp.float32)

            first, second, other, _swapped = blocks_of(s)

            @pl.when(number_of(s) < off_pairs)
            def _():
                kept = masked(total, first, second)
                res[s, 0] = kept.astype(res.dtype)
                res[s, 1] = (-swap_rows(kept, size)).astype(res.dtype)

            @pl.when(number_of(s) >= off_pairs)
            def _():
                res[s, 0] = masked(unpack_rows(total[:half], size), first, first).astype(res.dtype)
                res[s, 1] = masked(unpack_rows(total[half:], size), other, other).astype(res.dtype)

            deliver(s, "start")

    for source in range(n):
        remote(found.at[source], found.at[source], o_send.at[0, 0, 0], o_recv.at[source],
               col=source).wait_recv()

    whole = jnp.concatenate([found[source].astype(f32) for source in range(n)], axis=1)
    for i in range(size):
        out_ref[i] = -whole[i * size : (i + 1) * size].astype(out_ref.dtype)

    for s in range(slots):
        @pl.when((s * n + mine < per_rep) & (number_of(s) < numbers))
        def _():
            deliver(s, "wait")
    for q in range(per_rep):
        @pl.when(owner(q) != r)
        def _():
            to_owner(q).wait_send()
    for off in range(1, reps):
        swap_reps(off).wait_send()

    @pl.loop(0, kb)
    def _(k):
        for off in range(1, n):
            shuffle(k, off).wait_send()
        for c in range(n):
            if c > 0:
                @pl.when((z <= c) & (z > 0))
                def _():
                    to_left(k, c).wait_send()
            if c < n - 1:
                @pl.when((z >= c) & (z < n - 1))
                def _():
                    to_right(k, c).wait_send()

    for m in range(-(-kb // 2)):
        for c in range(n):
            if c > 0:
                @pl.when((z <= c) & (z > 0))
                def _():
                    g_left(m, c).wait_send()
            if c < n - 1:
                @pl.when((z >= c) & (z < n - 1))
                def _():
                    g_right(m, c).wait_send()


def ladder_blocks(amplitudes, integrals, occ_offsets, slab, n, reps):
    size, kb, _, pairs = amplitudes.shape
    rows, width = size * size, pairs // n
    slab_rows = integrals.shape[1]
    numbers = n * (n - 1) // 2 + -(-n // 2)
    chunks = -(-kb // 2)
    per_rep = -(-numbers // reps)
    slots = -(-per_rep // n)
    bf16, dma = jnp.bfloat16, pltpu.SemaphoreType.DMA
    return pl.pallas_call(
        functools.partial(kernel, n, reps, size),
        out_shape=jax.ShapeDtypeStruct((size, size, n * slab_rows), bf16),
        in_specs=[
            pl.BlockSpec(memory_space=pl.ANY),
            pl.BlockSpec(memory_space=pl.ANY),
            pl.BlockSpec(memory_space=pltpu.SMEM),
            pl.BlockSpec(memory_space=pltpu.SMEM),
        ],
        out_specs=pl.BlockSpec(memory_space=pltpu.VMEM),
        scratch_shapes=[
            pltpu.VMEM(amplitudes.shape[:1] + (kb, size, pairs), bf16),
            pltpu.VMEM((n, kb, rows, width), bf16),
            pltpu.VMEM((n, rows, slab_rows), bf16),
            pltpu.VMEM((kb, n, n, rows, width), bf16),
            pltpu.VMEM((n, chunks, rows, width), bf16),
            pltpu.VMEM((reps * per_rep, rows, width), bf16),
            pltpu.VMEM((kb, slab_rows, width), bf16),
            pltpu.VMEM((slab_rows, reps * per_rep * rows), jnp.float32),
            pltpu.VMEM((reps, per_rep, rows, slab_rows), bf16),
            pltpu.VMEM((max(reps - 1, 1), per_rep, rows, slab_rows), bf16),
            pltpu.VMEM((per_rep, rows, slab_rows), bf16),
            pltpu.VMEM((slots, n, rows, slab_rows), bf16),
            pltpu.VMEM((slots, 2, rows, slab_rows), bf16),
            dma,
            dma((kb,)),
            dma((kb, n - 1)),
            dma((kb, n - 1)),
            dma((kb, n)),
            dma((kb, n)),
            dma((kb, n)),
            dma((chunks, n)),
            dma((chunks, n)),
            dma((chunks, n)),
            dma((max(reps - 1, 1),)),
            dma((max(reps - 1, 1),)),
            dma((per_rep,)),
            dma((slots, n)),
            dma((slots, reps, 2)),
            dma((n,)),
        ],
        compiler_params=pltpu.CompilerParams(
            collective_id=0, has_side_effects=True, vmem_limit_bytes=56 * 1024 * 1024),
        name="ladder_blocks",
    )(amplitudes, integrals, occ_offsets, slab)


def shards(n, reps, amplitudes, integrals, occ_offsets, slab):
    return -ladder_blocks(
        jnp.transpose(amplitudes, (0, 2, 1, 3)), jnp.transpose(integrals, (1, 0, 2)),
        occ_offsets, slab, n, reps)


def solution(mesh):
    placed = (P("row", "col", "rep", None), P("col", "rep", "row"), P(), P())
    n, reps = mesh.shape["row"], mesh.shape["rep"]
    assert mesh.shape["col"] == n
    return jax.shard_map(
        functools.partial(shards, n, reps), mesh=mesh, in_specs=placed,
        out_specs=P("row", "col", None), check_vma=False
    )
```

```python
import functools

import jax
import jax.numpy as jnp
from jax import lax
from jax.experimental import pallas as pl
from jax.experimental.pallas import tpu as pltpu
from jax.sharding import PartitionSpec as P

MESH = pl.DeviceIdType.MESH


def pair_start(first, n):
    return first * (n - 1) - first * (first - 1) // 2


def pack_rows(block, size):
    above = [block[i * size + i + 1 : (i + 1) * size] for i in range(size - 1)]
    rest = size * size // 2 - size * (size - 1) // 2
    return jnp.concatenate(above + [jnp.zeros_like(block[:rest])], axis=0)


def row_orders(size):
    rows = size * size
    row = lax.broadcasted_iota(jnp.int32, (rows, rows), 0)
    column = lax.broadcasted_iota(jnp.int32, (rows, rows), 1)
    i = sum((row >= t * size).astype(jnp.int32) for t in range(1, size))
    j = row - size * i
    low, high = jnp.minimum(i, j), jnp.maximum(i, j)
    at = low * size + high - low - 1 - sum(jnp.where(low >= t, t, 0) for t in range(1, size))
    sign = jnp.where(i < j, 1.0, -1.0)

    def packed(start):
        return jnp.where((i != j) & (column == at + start), sign, 0.0)

    same = jnp.where(row == column, 1.0, 0.0)
    swapped = jnp.where(column == j * size + i, 1.0, 0.0)
    return same, swapped, packed(0), packed(rows // 2)


def kernel(n, reps, size, a_hbm, v_hbm, occ_ref, slab_ref, out_ref, a_ref, s_ref, found, x, g, dd, v, acc, pb, rrecv, qb, rowrecv, res,
           la, lv, a_send, a_recv, l_send, r_send, x_recv, gl_send, gr_send, g_recv, p_send, p_recv, q_send, q_recv,
           o_send, o_recv):
    kb = s_ref.shape[1]
    f32 = jnp.float32
    per_rep = pb.shape[1]
    slots = res.shape[0]
    off_pairs = n * (n - 1) // 2
    numbers = off_pairs + -(-n // 2)
    half = s_ref.shape[2] // 2
    width = s_ref.shape[3]
    piece = v.shape[2]
    same, swapped_rows, packed_first, packed_second = row_orders(size)

    def reorder(matrix, block):
        return jnp.dot(matrix.astype(jnp.bfloat16), block, preferred_element_type=f32)
    half_width = min(-(-width // 256) * 128, width)
    r, z, p = lax.axis_index("row"), lax.axis_index("col"), lax.axis_index("rep")

    def remote(src, dst, send, recv, **where):
        target = {"row": r, "col": z, "rep": p, **where}
        return pltpu.make_async_remote_copy(
            src_ref=src, dst_ref=dst, send_sem=send, recv_sem=recv,
            device_id=(target["row"], target["col"], target["rep"]), device_id_type=MESH)

    fetch = pltpu.make_async_copy(a_hbm, a_ref, la)
    fetch.start()
    for k in range(kb):
        pltpu.make_async_copy(v_hbm.at[k], v.at[k], lv.at[k]).start()

    barrier = pltpu.get_barrier_semaphore()
    devices = n * n * reps
    me = (r * n + z) * reps + p

    @pl.loop(1, devices)
    def _(off):
        other = lax.rem(me + off, devices)
        pl.semaphore_signal(
            barrier, inc=1,
            device_id=(other // (n * reps), lax.rem(other // reps, n), lax.rem(other, reps)),
            device_id_type=MESH)

    def shuffle(k, off):
        dest = lax.rem(r + off, n)
        return remote(s_ref.at[dest, k], x.at[k, z, r], a_send.at[k, off - 1],
                      a_recv.at[k, off - 1], row=dest)

    def shuffled(k, off):
        source = lax.rem(r + n - off, n)
        return remote(s_ref.at[source, k], x.at[k, z, source], a_send.at[k, off - 1],
                      a_recv.at[k, off - 1], row=source)

    def stage(k):
        natural = jnp.concatenate([a_ref[i, k].astype(f32) for i in range(size)], axis=0)
        order = jnp.where(r < z, same, jnp.where(r > z, swapped_rows, same - swapped_rows))
        staged = reorder(order, natural.astype(s_ref.dtype)).astype(s_ref.dtype)
        for dest in range(n):
            start = dest * piece // 128 * 128
            stop = min(start + width, staged.shape[1])
            if stop - start < width:
                s_ref[dest, k, :, pl.ds(width - 256, 256)] = jnp.zeros(
                    (size * size, 256), s_ref.dtype)
            s_ref[dest, k, :, pl.ds(0, stop - start)] = staged[:, start:stop]

    acc[...] = jnp.zeros_like(acc)
    fetch.wait()
    stage(0)
    if reps * per_rep != numbers:
        dd[...] = jnp.zeros_like(dd)
    pl.semaphore_wait(barrier, devices - 1)
    def send_shuffle(k):
        for off in range(1, n):
            shuffle(k, off).start()
        x[k, z, r] = s_ref[r, k]

    send_shuffle(0)
    if kb > 1:
        stage(1)
        send_shuffle(1)

    left, right = lax.max(z - 1, 0), lax.min(z + 1, n - 1)

    def to_left(k, c):
        part = x.at[k, c, pl.ds(0, c)]
        return remote(part, part, l_send.at[k, c], x_recv.at[k, c], col=left)

    def to_right(k, c):
        part = x.at[k, c, pl.ds(c + 1, n - 1 - c)]
        return remote(part, part, r_send.at[k, c], x_recv.at[k, c], col=right)

    def diagonal(m, c):
        return g.at[c, m] if 2 * m + 1 < kb else g.at[c, m, :, pl.ds(0, half_width)]

    def g_left(m, c):
        return remote(diagonal(m, c), diagonal(m, c), gl_send.at[m, c], g_recv.at[m, c], col=left)

    def g_right(m, c):
        return remote(diagonal(m, c), diagonal(m, c), gr_send.at[m, c], g_recv.at[m, c], col=right)

    def pack(m):
        first = pack_rows(x[2 * m, z, z].astype(jnp.float32), size)
        if 2 * m + 1 < kb:
            second = pack_rows(x[2 * m + 1, z, z].astype(jnp.float32), size)
            g[z, m] = jnp.concatenate([first, second], axis=0).astype(g.dtype)
        else:
            tail = first[:, half_width:]
            if 2 * half_width > width:
                fill = jnp.zeros((half, 2 * half_width - width), jnp.float32)
                tail = jnp.concatenate([tail, fill], axis=1)
            g[z, m, :, pl.ds(0, half_width)] = jnp.concatenate(
                [first[:, :half_width], tail], axis=0).astype(g.dtype)

    def unpacked(k, c):
        m = k // 2
        if 2 * m + 1 < kb:
            both = g[c, m].astype(jnp.float32)
            return both[:half] if k % 2 == 0 else both[half:]
        both = g[c, m, :, pl.ds(0, half_width)].astype(jnp.float32)
        return jnp.concatenate([both[:half], both[half:, : width - half_width]], axis=1)

    for k in range(kb):
        for off in range(1, n):
            shuffled(k, off).wait_recv()
        for c in range(n):
            @pl.when(z == c)
            def _():
                if c > 0:
                    to_left(k, c).start()
                if c < n - 1:
                    to_right(k, c).start()
        if k + 2 < kb:
            stage(k + 2)
            send_shuffle(k + 2)
        if k % 2 == 1 or k == kb - 1:
            pack(k // 2)
            for c in range(n):
                @pl.when(z == c)
                def _():
                    if c > 0:
                        g_left(k // 2, c).start()
                    if c < n - 1:
                        g_right(k // 2, c).start()

    def slot_of(number):
        return number % reps * per_rep + number // reps

    def assemble(k, first, second):
        slot = slot_of(pair_start(first, n) + second - first - 1)

        @pl.when(z <= first)
        def _():
            dd[slot] = x[k, second, first]

        @pl.when(z >= second)
        def _():
            dd[slot] = x[k, first, second]

        @pl.when((z > first) & (z < second))
        def _():
            dd[slot] = (x[k, second, first].astype(f32)
                        - x[k, first, second].astype(f32)).astype(dd.dtype)

    def arrivals(k, d):
        for c in range(n):
            if c >= d:
                @pl.when(z == c - d)
                def _():
                    to_left(k, c).wait_recv()
                    x[k, c, c - d] = (x[k, c, c - d].astype(f32)
                                      - x[k, c - d, c].astype(f32)).astype(x.dtype)
                    if c > d:
                        to_left(k, c).start()
                    for m in range(-(-kb // 2)):
                        @pl.when(k == 2 * m)
                        def _():
                            g_left(m, c).wait_recv()
                            if c > d:
                                g_left(m, c).start()
            if c + d < n:
                @pl.when(z == c + d)
                def _():
                    to_right(k, c).wait_recv()
                    x[k, c, c + d] = (x[k, c + d, c].astype(f32)
                                      - x[k, c, c + d].astype(f32)).astype(x.dtype)
                    if c + d < n - 1:
                        to_right(k, c).start()
                    for m in range(-(-kb // 2)):
                        @pl.when(k == 2 * m)
                        def _():
                            g_right(m, c).wait_recv()
                            if c + d < n - 1:
                                g_right(m, c).start()

    def multiply(k):
        @pl.loop(0, n - 1)
        def _(first):
            @pl.loop(first + 1, n)
            def _(second):
                assemble(k, first, second)

        for now in range(kb):
            @pl.when(k == now)
            def _():
                for c in range(0, n, 2):
                    one = unpacked(now, c)
                    two = unpacked(now, c + 1) if c + 1 < n else jnp.zeros_like(one)
                    dd[slot_of(off_pairs + c // 2)] = jnp.concatenate(
                        [one, two], axis=0).astype(dd.dtype)

        pltpu.make_async_copy(v_hbm.at[k], v.at[k], lv.at[k]).wait()
        wide = dd[...].reshape(acc.shape[1], width).astype(f32)
        shift = lax.rem(width - lax.rem(r * piece, 128), width)
        aligned = pltpu.roll(wide, shift, 1)[:, :piece].astype(dd.dtype)
        acc[...] += lax.dot_general(
            v[k], aligned,
            (((1,), (1,)), ((), ())), preferred_element_type=f32)

    last = lax.max(z, n - 1 - z)
    for d in range(1, n):
        @pl.loop(0, kb)
        def _(k):
            arrivals(k, d)
            if 2 * d >= n - 1:
                @pl.when(d == last)
                def _():
                    multiply(k)

    pb[...] = acc[...].T.reshape(pb.shape).astype(pb.dtype)

    def swap_reps(off):
        other = lax.rem(p + off, reps)
        return remote(pb.at[other], rrecv.at[off - 1], p_send.at[off - 1], p_recv.at[off - 1],
                      rep=other)

    for off in range(1, reps):
        swap_reps(off).start()
    for off in range(1, reps):
        swap_reps(off).wait_recv()

    flip = lax.rem(p, 2)

    def owner(q):
        return lax.rem(q, n) * (1 - 2 * flip) + (n - 1) * flip

    def to_owner(q):
        return remote(qb.at[q], rowrecv.at[q // n, r], q_send.at[q],
                      q_recv.at[q // n, r], row=owner(q))

    for q in range(per_rep):
        total = pb[p, q].astype(jnp.float32)
        for off in range(1, reps):
            total += rrecv[off - 1, q].astype(jnp.float32)
        qb[q] = total.astype(qb.dtype)

        @pl.when(owner(q) != r)
        def _():
            to_owner(q).start()

    mine = r * (1 - 2 * flip) + (n - 1) * flip

    place = lax.broadcasted_iota(jnp.int32, (size * size, 128), 0)
    place_i = sum((place >= t * size).astype(jnp.int32) for t in range(1, size))
    place_j = place - size * place_i
    target = jnp.bitwise_xor(slab_ref[0], slab_ref[1])

    def labels(orbitals):
        return sum((orbitals >= occ_ref[t]).astype(jnp.int32)
                   for t in range(1, occ_ref.shape[0] - 1))

    def masked(block, first, second):
        mixed = jnp.bitwise_xor(labels(first * size + place_i), labels(second * size + place_j))
        allowed = (mixed == target).astype(f32)[:, :1]
        return jnp.where(jnp.broadcast_to(allowed, block.shape) > 0, block, jnp.zeros_like(block))

    def number_of(s):
        return (s * n + mine) * reps + p

    def blocks_of(s):
        number = number_of(s)
        first = 0
        for t in range(1, n - 1):
            first = first + (number >= pair_start(t, n)).astype(jnp.int32)
        second = number - pair_start(first, n) + first + 1
        even = 2 * (number - off_pairs)
        apart = number < off_pairs
        first, other = jnp.where(apart, first, even), jnp.where(apart, first, even + 1)
        second, swapped = jnp.where(apart, second, even), jnp.where(apart, second, even + 1)
        return first, second, other, swapped

    def deliver(s, do):
        first, second, other, swapped = blocks_of(s)
        for rep in range(reps):
            for t, (row, col) in enumerate(((first, second), (swapped, other))):
                local = (row == r) & (col == z) & (p == rep)
                wanted = (row < n) & (col < n)

                @pl.when(wanted & local)
                def _():
                    if do == "start":
                        pltpu.make_async_copy(res.at[s, t], found.at[z], o_recv.at[z]).start()

                @pl.when(wanted & jnp.logical_not(local))
                def _():
                    copy = remote(res.at[s, t], found.at[z], o_send.at[s, rep, t],
                                  o_recv.at[z], row=row, col=col, rep=rep)
                    if do == "start":
                        copy.start()
                    else:
                        copy.wait_send()

    for s in range(slots):
        @pl.when((s * n + mine < per_rep) & (number_of(s) < numbers))
        def _():
            total = qb[s * n + mine].astype(jnp.float32)
            for off in range(1, n):
                source = lax.rem(r + off, n)
                remote(rowrecv.at[s, source], rowrecv.at[s, source], q_send.at[0],
                       q_recv.at[s, source], row=source).wait_recv()
                total += rowrecv[s, source].astype(jnp.float32)

            first, second, other, swapped = blocks_of(s)
            apart = number_of(s) < off_pairs
            rounded = total.astype(res.dtype)
            one = reorder(jnp.where(apart, same, packed_first), rounded)
            two = reorder(jnp.where(apart, -swapped_rows, packed_second), rounded)
            res[s, 0] = masked(one, first, second).astype(res.dtype)
            res[s, 1] = masked(two, swapped, other).astype(res.dtype)
            deliver(s, "start")

    for source in range(n):
        remote(found.at[source], found.at[source], o_send.at[0, 0, 0], o_recv.at[source],
               col=source).wait_recv()

    whole = jnp.concatenate([found[source].astype(f32) for source in range(n)], axis=1)
    for i in range(size):
        out_ref[i] = -whole[i * size : (i + 1) * size].astype(out_ref.dtype)

    for s in range(slots):
        @pl.when((s * n + mine < per_rep) & (number_of(s) < numbers))
        def _():
            deliver(s, "wait")
    for q in range(per_rep):
        @pl.when(owner(q) != r)
        def _():
            to_owner(q).wait_send()
    for off in range(1, reps):
        swap_reps(off).wait_send()

    @pl.loop(0, kb)
    def _(k):
        for off in range(1, n):
            shuffle(k, off).wait_send()
        for c in range(n):
            if c > 0:
                @pl.when((z <= c) & (z > 0))
                def _():
                    to_left(k, c).wait_send()
            if c < n - 1:
                @pl.when((z >= c) & (z < n - 1))
                def _():
                    to_right(k, c).wait_send()

    for m in range(-(-kb // 2)):
        for c in range(n):
            if c > 0:
                @pl.when((z <= c) & (z > 0))
                def _():
                    g_left(m, c).wait_send()
            if c < n - 1:
                @pl.when((z >= c) & (z < n - 1))
                def _():
                    g_right(m, c).wait_send()


def ladder_blocks(amplitudes, integrals, occ_offsets, slab, n, reps):
    size, kb, _, pairs = amplitudes.shape
    rows, piece = size * size, pairs // n
    width = max(-(-(t * piece % 128 + piece) // 128) * 128 for t in range(n))
    slab_rows = integrals.shape[1]
    numbers = n * (n - 1) // 2 + -(-n // 2)
    chunks = -(-kb // 2)
    per_rep = -(-numbers // reps)
    slots = -(-per_rep // n)
    bf16, dma = jnp.bfloat16, pltpu.SemaphoreType.DMA
    return pl.pallas_call(
        functools.partial(kernel, n, reps, size),
        out_shape=jax.ShapeDtypeStruct((size, size, n * slab_rows), bf16),
        in_specs=[
            pl.BlockSpec(memory_space=pl.ANY),
            pl.BlockSpec(memory_space=pl.ANY),
            pl.BlockSpec(memory_space=pltpu.SMEM),
            pl.BlockSpec(memory_space=pltpu.SMEM),
        ],
        out_specs=pl.BlockSpec(memory_space=pltpu.VMEM),
        scratch_shapes=[
            pltpu.VMEM(amplitudes.shape[:1] + (kb, size, pairs), bf16),
            pltpu.VMEM((n, kb, rows, width), bf16),
            pltpu.VMEM((n, rows, slab_rows), bf16),
            pltpu.VMEM((kb, n, n, rows, width), bf16),
            pltpu.VMEM((n, chunks, rows, width), bf16),
            pltpu.VMEM((reps * per_rep, rows, width), bf16),
            pltpu.VMEM((kb, slab_rows, piece), bf16),
            pltpu.VMEM((slab_rows, reps * per_rep * rows), jnp.float32),
            pltpu.VMEM((reps, per_rep, rows, slab_rows), bf16),
            pltpu.VMEM((max(reps - 1, 1), per_rep, rows, slab_rows), bf16),
            pltpu.VMEM((per_rep, rows, slab_rows), bf16),
            pltpu.VMEM((slots, n, rows, slab_rows), bf16),
            pltpu.VMEM((slots, 2, rows, slab_rows), bf16),
            dma,
            dma((kb,)),
            dma((kb, n - 1)),
            dma((kb, n - 1)),
            dma((kb, n)),
            dma((kb, n)),
            dma((kb, n)),
            dma((chunks, n)),
            dma((chunks, n)),
            dma((chunks, n)),
            dma((max(reps - 1, 1),)),
            dma((max(reps - 1, 1),)),
            dma((per_rep,)),
            dma((slots, n)),
            dma((slots, reps, 2)),
            dma((n,)),
        ],
        compiler_params=pltpu.CompilerParams(
            collective_id=0, has_side_effects=True, vmem_limit_bytes=56 * 1024 * 1024),
        name="ladder_blocks",
    )(amplitudes, integrals, occ_offsets, slab)


def shards(n, reps, amplitudes, integrals, occ_offsets, slab):
    return -ladder_blocks(
        jnp.transpose(amplitudes, (0, 2, 1, 3)), jnp.transpose(integrals, (1, 0, 2)),
        occ_offsets, slab, n, reps)


def solution(mesh):
    placed = (P("row", "col", "rep", None), P("col", "rep", "row"), P(), P())
    n, reps = mesh.shape["row"], mesh.shape["rep"]
    assert mesh.shape["col"] == n
    return jax.shard_map(
        functools.partial(shards, n, reps), mesh=mesh, in_specs=placed,
        out_specs=P("row", "col", None), check_vma=False
    )
```

```python
import functools

import jax
import jax.numpy as jnp
from jax import lax
from jax.experimental import pallas as pl
from jax.experimental.pallas import tpu as pltpu
from jax.sharding import PartitionSpec as P

MESH = pl.DeviceIdType.MESH


def pair_start(first, n):
    return first * (n - 1) - first * (first - 1) // 2


def pack_rows(block, size):
    above = [block[i * size + i + 1 : (i + 1) * size] for i in range(size - 1)]
    rest = size * size // 2 - size * (size - 1) // 2
    return jnp.concatenate(above + [jnp.zeros_like(block[:rest])], axis=0)


def row_orders(size):
    rows = size * size
    row = lax.broadcasted_iota(jnp.int32, (rows, rows), 0)
    column = lax.broadcasted_iota(jnp.int32, (rows, rows), 1)
    i = sum((row >= t * size).astype(jnp.int32) for t in range(1, size))
    j = row - size * i
    low, high = jnp.minimum(i, j), jnp.maximum(i, j)
    at = low * size + high - low - 1 - sum(jnp.where(low >= t, t, 0) for t in range(1, size))
    sign = jnp.where(i < j, 1.0, -1.0)

    def packed(start):
        return jnp.where((i != j) & (column == at + start), sign, 0.0)

    same = jnp.where(row == column, 1.0, 0.0)
    swapped = jnp.where(column == j * size + i, 1.0, 0.0)
    return same, swapped, packed(0), packed(rows // 2)


def kernel(n, reps, size, a_hbm, v_hbm, occ_ref, slab_ref, out_ref, a_ref, s_ref, found, x, g, dd, v, acc, pb, rrecv, qb, rowrecv, res,
           la, lv, a_send, a_recv, l_send, r_send, x_recv, gl_send, gr_send, g_recv, p_send, p_recv, q_send, q_recv,
           o_send, o_recv):
    kb = s_ref.shape[1]
    f32 = jnp.float32
    per_rep = pb.shape[1]
    slots = res.shape[0]
    off_pairs = n * (n - 1) // 2
    numbers = off_pairs + -(-n // 2)
    half = s_ref.shape[2] // 2
    width = s_ref.shape[3]
    piece = v.shape[2]
    same, swapped_rows, packed_first, packed_second = row_orders(size)

    def reorder(matrix, block):
        return jnp.dot(matrix.astype(jnp.bfloat16), block, preferred_element_type=f32)
    half_width = min(-(-width // 256) * 128, width)
    r, z, p = lax.axis_index("row"), lax.axis_index("col"), lax.axis_index("rep")

    def remote(src, dst, send, recv, **where):
        target = {"row": r, "col": z, "rep": p, **where}
        return pltpu.make_async_remote_copy(
            src_ref=src, dst_ref=dst, send_sem=send, recv_sem=recv,
            device_id=(target["row"], target["col"], target["rep"]), device_id_type=MESH)

    fetch = pltpu.make_async_copy(a_hbm, a_ref, la)
    fetch.start()

    barrier = pltpu.get_barrier_semaphore()

    def greet(**where):
        target = {"row": r, "col": z, "rep": p, **where}
        pl.semaphore_signal(
            barrier, inc=1, device_id=(target["row"], target["col"], target["rep"]),
            device_id_type=MESH)

    for off in range(1, n):
        greet(row=lax.rem(r + off, n))
    for off in range(1, reps):
        greet(rep=lax.rem(p + off, reps))

    @pl.when(z > 0)
    def _():
        greet(col=lax.max(z - 1, 0))

    @pl.when(z < n - 1)
    def _():
        greet(col=lax.min(z + 1, n - 1))

    def shuffle(k, off):
        dest = lax.rem(r + off, n)
        return remote(s_ref.at[dest, k], x.at[k, z, r], a_send.at[k, off - 1],
                      a_recv.at[k, off - 1], row=dest)

    def shuffled(k, off):
        source = lax.rem(r + n - off, n)
        return remote(s_ref.at[source, k], x.at[k, z, source], a_send.at[k, off - 1],
                      a_recv.at[k, off - 1], row=source)

    def stage(k):
        natural = jnp.concatenate([a_ref[i, k].astype(f32) for i in range(size)], axis=0)
        order = jnp.where(r < z, same, jnp.where(r > z, swapped_rows, same - swapped_rows))
        staged = reorder(order, natural.astype(s_ref.dtype)).astype(s_ref.dtype)
        for dest in range(n):
            start = dest * piece // 128 * 128
            stop = min(start + width, staged.shape[1])
            if stop - start < width:
                s_ref[dest, k, :, pl.ds(width - 256, 256)] = jnp.zeros(
                    (size * size, 256), s_ref.dtype)
            s_ref[dest, k, :, pl.ds(0, stop - start)] = staged[:, start:stop]

    acc[...] = jnp.zeros_like(acc)
    fetch.wait()
    stage(0)
    if reps * per_rep != numbers:
        dd[...] = jnp.zeros_like(dd)
    beside = (z > 0).astype(jnp.int32) + (z < n - 1).astype(jnp.int32)
    pl.semaphore_wait(barrier, n - 1 + reps - 1 + beside)
    def send_shuffle(k):
        for off in range(1, n):
            shuffle(k, off).start()
        x[k, z, r] = s_ref[r, k]

    send_shuffle(0)
    if kb > 1:
        stage(1)
        send_shuffle(1)

    left, right = lax.max(z - 1, 0), lax.min(z + 1, n - 1)

    def to_left(k, c):
        part = x.at[k, c, pl.ds(0, c)]
        return remote(part, part, l_send.at[k, c], x_recv.at[k, c], col=left)

    def to_right(k, c):
        part = x.at[k, c, pl.ds(c + 1, n - 1 - c)]
        return remote(part, part, r_send.at[k, c], x_recv.at[k, c], col=right)

    def diagonal(m, c):
        return g.at[c, m] if 2 * m + 1 < kb else g.at[c, m, :, pl.ds(0, half_width)]

    def g_left(m, c):
        return remote(diagonal(m, c), diagonal(m, c), gl_send.at[m, c], g_recv.at[m, c], col=left)

    def g_right(m, c):
        return remote(diagonal(m, c), diagonal(m, c), gr_send.at[m, c], g_recv.at[m, c], col=right)

    def pack(m):
        first = pack_rows(x[2 * m, z, z].astype(jnp.float32), size)
        if 2 * m + 1 < kb:
            second = pack_rows(x[2 * m + 1, z, z].astype(jnp.float32), size)
            g[z, m] = jnp.concatenate([first, second], axis=0).astype(g.dtype)
        else:
            tail = first[:, half_width:]
            if 2 * half_width > width:
                fill = jnp.zeros((half, 2 * half_width - width), jnp.float32)
                tail = jnp.concatenate([tail, fill], axis=1)
            g[z, m, :, pl.ds(0, half_width)] = jnp.concatenate(
                [first[:, :half_width], tail], axis=0).astype(g.dtype)

    def unpacked(k, c):
        m = k // 2
        if 2 * m + 1 < kb:
            both = g[c, m].astype(jnp.float32)
            return both[:half] if k % 2 == 0 else both[half:]
        both = g[c, m, :, pl.ds(0, half_width)].astype(jnp.float32)
        return jnp.concatenate([both[:half], both[half:, : width - half_width]], axis=1)

    for k in range(kb):
        for off in range(1, n):
            shuffled(k, off).wait_recv()
        for c in range(n):
            @pl.when(z == c)
            def _():
                if c > 0:
                    to_left(k, c).start()
                if c < n - 1:
                    to_right(k, c).start()
        pltpu.make_async_copy(v_hbm.at[k], v.at[k], lv.at[k]).start()
        if k + 2 < kb:
            stage(k + 2)
            send_shuffle(k + 2)
        if k % 2 == 1 or k == kb - 1:
            pack(k // 2)
            for c in range(n):
                @pl.when(z == c)
                def _():
                    if c > 0:
                        g_left(k // 2, c).start()
                    if c < n - 1:
                        g_right(k // 2, c).start()

    def slot_of(number):
        return number % reps * per_rep + number // reps

    def assemble(k, first, second):
        slot = slot_of(pair_start(first, n) + second - first - 1)

        @pl.when(z <= first)
        def _():
            dd[slot] = x[k, second, first]

        @pl.when(z >= second)
        def _():
            dd[slot] = x[k, first, second]

        @pl.when((z > first) & (z < second))
        def _():
            dd[slot] = (x[k, second, first].astype(f32)
                        - x[k, first, second].astype(f32)).astype(dd.dtype)

    def arrivals(k, d):
        for c in range(n):
            if c >= d:
                @pl.when(z == c - d)
                def _():
                    to_left(k, c).wait_recv()
                    x[k, c, c - d] = (x[k, c, c - d].astype(f32)
                                      - x[k, c - d, c].astype(f32)).astype(x.dtype)
                    if c > d:
                        to_left(k, c).start()
                    for m in range(-(-kb // 2)):
                        @pl.when(k == 2 * m)
                        def _():
                            g_left(m, c).wait_recv()
                            if c > d:
                                g_left(m, c).start()
            if c + d < n:
                @pl.when(z == c + d)
                def _():
                    to_right(k, c).wait_recv()
                    x[k, c, c + d] = (x[k, c + d, c].astype(f32)
                                      - x[k, c, c + d].astype(f32)).astype(x.dtype)
                    if c + d < n - 1:
                        to_right(k, c).start()
                    for m in range(-(-kb // 2)):
                        @pl.when(k == 2 * m)
                        def _():
                            g_right(m, c).wait_recv()
                            if c + d < n - 1:
                                g_right(m, c).start()

    def multiply(k):
        @pl.loop(0, n - 1)
        def _(first):
            @pl.loop(first + 1, n)
            def _(second):
                assemble(k, first, second)

        for now in range(kb):
            @pl.when(k == now)
            def _():
                for c in range(0, n, 2):
                    one = unpacked(now, c)
                    two = unpacked(now, c + 1) if c + 1 < n else jnp.zeros_like(one)
                    dd[slot_of(off_pairs + c // 2)] = jnp.concatenate(
                        [one, two], axis=0).astype(dd.dtype)

        pltpu.make_async_copy(v_hbm.at[k], v.at[k], lv.at[k]).wait()
        wide = dd[...].reshape(acc.shape[1], width).astype(f32)
        shift = lax.rem(width - lax.rem(r * piece, 128), width)
        aligned = pltpu.roll(wide, shift, 1)[:, :piece].astype(dd.dtype)
        acc[...] += lax.dot_general(
            v[k], aligned,
            (((1,), (1,)), ((), ())), preferred_element_type=f32)

    last = lax.max(z, n - 1 - z)
    for d in range(1, n):
        @pl.loop(0, kb)
        def _(k):
            arrivals(k, d)
            if 2 * d >= n - 1:
                @pl.when(d == last)
                def _():
                    multiply(k)

    pb[...] = acc[...].T.reshape(pb.shape).astype(pb.dtype)

    def swap_reps(off):
        other = lax.rem(p + off, reps)
        return remote(pb.at[other], rrecv.at[off - 1], p_send.at[off - 1], p_recv.at[off - 1],
                      rep=other)

    for off in range(1, reps):
        swap_reps(off).start()
    for off in range(1, reps):
        swap_reps(off).wait_recv()

    flip = lax.rem(p, 2)

    def owner(q):
        return lax.rem(q, n) * (1 - 2 * flip) + (n - 1) * flip

    def to_owner(q):
        return remote(qb.at[q], rowrecv.at[q // n, r], q_send.at[q],
                      q_recv.at[q // n, r], row=owner(q))

    for q in range(per_rep):
        total = pb[p, q].astype(jnp.float32)
        for off in range(1, reps):
            total += rrecv[off - 1, q].astype(jnp.float32)
        qb[q] = total.astype(qb.dtype)

        @pl.when(owner(q) != r)
        def _():
            to_owner(q).start()

    mine = r * (1 - 2 * flip) + (n - 1) * flip

    place = lax.broadcasted_iota(jnp.int32, (size * size, 128), 0)
    place_i = sum((place >= t * size).astype(jnp.int32) for t in range(1, size))
    place_j = place - size * place_i
    target = jnp.bitwise_xor(slab_ref[0], slab_ref[1])

    def labels(orbitals):
        return sum((orbitals >= occ_ref[t]).astype(jnp.int32)
                   for t in range(1, occ_ref.shape[0] - 1))

    def masked(block, first, second):
        mixed = jnp.bitwise_xor(labels(first * size + place_i), labels(second * size + place_j))
        allowed = (mixed == target).astype(f32)[:, :1]
        return jnp.where(jnp.broadcast_to(allowed, block.shape) > 0, block, jnp.zeros_like(block))

    def number_of(s):
        return (s * n + mine) * reps + p

    def blocks_of(s):
        number = number_of(s)
        first = 0
        for t in range(1, n - 1):
            first = first + (number >= pair_start(t, n)).astype(jnp.int32)
        second = number - pair_start(first, n) + first + 1
        even = 2 * (number - off_pairs)
        apart = number < off_pairs
        first, other = jnp.where(apart, first, even), jnp.where(apart, first, even + 1)
        second, swapped = jnp.where(apart, second, even), jnp.where(apart, second, even + 1)
        return first, second, other, swapped

    def deliver(s, do):
        first, second, other, swapped = blocks_of(s)
        for rep in range(reps):
            for t, (row, col) in enumerate(((first, second), (swapped, other))):
                local = (row == r) & (col == z) & (p == rep)
                wanted = (row < n) & (col < n)

                @pl.when(wanted & local)
                def _():
                    if do == "start":
                        pltpu.make_async_copy(res.at[s, t], found.at[z], o_recv.at[z]).start()

                @pl.when(wanted & jnp.logical_not(local))
                def _():
                    copy = remote(res.at[s, t], found.at[z], o_send.at[s, rep, t],
                                  o_recv.at[z], row=row, col=col, rep=rep)
                    if do == "start":
                        copy.start()
                    else:
                        copy.wait_send()

    for s in range(slots):
        @pl.when((s * n + mine < per_rep) & (number_of(s) < numbers))
        def _():
            total = qb[s * n + mine].astype(jnp.float32)
            for off in range(1, n):
                source = lax.rem(r + off, n)
                remote(rowrecv.at[s, source], rowrecv.at[s, source], q_send.at[0],
                       q_recv.at[s, source], row=source).wait_recv()
                total += rowrecv[s, source].astype(jnp.float32)

            first, second, other, swapped = blocks_of(s)
            apart = number_of(s) < off_pairs
            rounded = total.astype(res.dtype)
            one = reorder(jnp.where(apart, same, packed_first), rounded)
            two = reorder(jnp.where(apart, -swapped_rows, packed_second), rounded)
            res[s, 0] = masked(one, first, second).astype(res.dtype)
            res[s, 1] = masked(two, swapped, other).astype(res.dtype)
            deliver(s, "start")

    for source in range(n):
        remote(found.at[source], found.at[source], o_send.at[0, 0, 0], o_recv.at[source],
               col=source).wait_recv()

    whole = jnp.concatenate([found[source].astype(f32) for source in range(n)], axis=1)
    for i in range(size):
        out_ref[i] = -whole[i * size : (i + 1) * size].astype(out_ref.dtype)

    for s in range(slots):
        @pl.when((s * n + mine < per_rep) & (number_of(s) < numbers))
        def _():
            deliver(s, "wait")
    for q in range(per_rep):
        @pl.when(owner(q) != r)
        def _():
            to_owner(q).wait_send()
    for off in range(1, reps):
        swap_reps(off).wait_send()

    @pl.loop(0, kb)
    def _(k):
        for off in range(1, n):
            shuffle(k, off).wait_send()
        for c in range(n):
            if c > 0:
                @pl.when((z <= c) & (z > 0))
                def _():
                    to_left(k, c).wait_send()
            if c < n - 1:
                @pl.when((z >= c) & (z < n - 1))
                def _():
                    to_right(k, c).wait_send()

    for m in range(-(-kb // 2)):
        for c in range(n):
            if c > 0:
                @pl.when((z <= c) & (z > 0))
                def _():
                    g_left(m, c).wait_send()
            if c < n - 1:
                @pl.when((z >= c) & (z < n - 1))
                def _():
                    g_right(m, c).wait_send()


def ladder_blocks(amplitudes, integrals, occ_offsets, slab, n, reps):
    size, kb, _, pairs = amplitudes.shape
    rows, piece = size * size, pairs // n
    width = max(-(-(t * piece % 128 + piece) // 128) * 128 for t in range(n))
    slab_rows = integrals.shape[1]
    numbers = n * (n - 1) // 2 + -(-n // 2)
    chunks = -(-kb // 2)
    per_rep = -(-numbers // reps)
    slots = -(-per_rep // n)
    bf16, dma = jnp.bfloat16, pltpu.SemaphoreType.DMA
    return pl.pallas_call(
        functools.partial(kernel, n, reps, size),
        out_shape=jax.ShapeDtypeStruct((size, size, n * slab_rows), bf16),
        in_specs=[
            pl.BlockSpec(memory_space=pl.ANY),
            pl.BlockSpec(memory_space=pl.ANY),
            pl.BlockSpec(memory_space=pltpu.SMEM),
            pl.BlockSpec(memory_space=pltpu.SMEM),
        ],
        out_specs=pl.BlockSpec(memory_space=pltpu.VMEM),
        scratch_shapes=[
            pltpu.VMEM(amplitudes.shape[:1] + (kb, size, pairs), bf16),
            pltpu.VMEM((n, kb, rows, width), bf16),
            pltpu.VMEM((n, rows, slab_rows), bf16),
            pltpu.VMEM((kb, n, n, rows, width), bf16),
            pltpu.VMEM((n, chunks, rows, width), bf16),
            pltpu.VMEM((reps * per_rep, rows, width), bf16),
            pltpu.VMEM((kb, slab_rows, piece), bf16),
            pltpu.VMEM((slab_rows, reps * per_rep * rows), jnp.float32),
            pltpu.VMEM((reps, per_rep, rows, slab_rows), bf16),
            pltpu.VMEM((max(reps - 1, 1), per_rep, rows, slab_rows), bf16),
            pltpu.VMEM((per_rep, rows, slab_rows), bf16),
            pltpu.VMEM((slots, n, rows, slab_rows), bf16),
            pltpu.VMEM((slots, 2, rows, slab_rows), bf16),
            dma,
            dma((kb,)),
            dma((kb, n - 1)),
            dma((kb, n - 1)),
            dma((kb, n)),
            dma((kb, n)),
            dma((kb, n)),
            dma((chunks, n)),
            dma((chunks, n)),
            dma((chunks, n)),
            dma((max(reps - 1, 1),)),
            dma((max(reps - 1, 1),)),
            dma((per_rep,)),
            dma((slots, n)),
            dma((slots, reps, 2)),
            dma((n,)),
        ],
        compiler_params=pltpu.CompilerParams(
            collective_id=0, has_side_effects=True, vmem_limit_bytes=56 * 1024 * 1024),
        name="ladder_blocks",
    )(amplitudes, integrals, occ_offsets, slab)


def shards(n, reps, amplitudes, integrals, occ_offsets, slab):
    return -ladder_blocks(
        jnp.transpose(amplitudes, (0, 2, 1, 3)), jnp.transpose(integrals, (1, 0, 2)),
        occ_offsets, slab, n, reps)


def solution(mesh):
    placed = (P("row", "col", "rep", None), P("col", "rep", "row"), P(), P())
    n, reps = mesh.shape["row"], mesh.shape["rep"]
    assert mesh.shape["col"] == n
    return jax.shard_map(
        functools.partial(shards, n, reps), mesh=mesh, in_specs=placed,
        out_specs=P("row", "col", None), check_vma=False
    )
```

```python
import functools

import jax
import jax.numpy as jnp
from jax import lax
from jax.experimental import pallas as pl
from jax.experimental.pallas import tpu as pltpu
from jax.sharding import PartitionSpec as P

MESH = pl.DeviceIdType.MESH


def pair_start(first, n):
    return first * (n - 1) - first * (first - 1) // 2


def pack_rows(block, size):
    above = [block[i * size + i + 1 : (i + 1) * size] for i in range(size - 1)]
    rest = size * size // 2 - size * (size - 1) // 2
    return jnp.concatenate(above + [jnp.zeros_like(block[:rest])], axis=0)


def row_orders(size):
    rows = size * size
    row = lax.broadcasted_iota(jnp.int32, (rows, rows), 0)
    column = lax.broadcasted_iota(jnp.int32, (rows, rows), 1)
    i = sum((row >= t * size).astype(jnp.int32) for t in range(1, size))
    j = row - size * i
    low, high = jnp.minimum(i, j), jnp.maximum(i, j)
    at = low * size + high - low - 1 - sum(jnp.where(low >= t, t, 0) for t in range(1, size))
    sign = jnp.where(i < j, 1.0, -1.0)

    def packed(start):
        return jnp.where((i != j) & (column == at + start), sign, 0.0)

    same = jnp.where(row == column, 1.0, 0.0)
    swapped = jnp.where(column == j * size + i, 1.0, 0.0)
    return same, swapped, packed(0), packed(rows // 2)


def kernel(n, reps, size, a_hbm, v_hbm, occ_ref, slab_ref, out_ref, a_ref, s_ref, found, x, g, dd, v, acc, pb, rrecv, qb, rowrecv, res,
           la, lv, a_send, a_recv, l_send, r_send, x_recv, gl_send, gr_send, g_recv, p_send, p_recv, q_send, q_recv,
           o_send, o_recv):
    kb = s_ref.shape[1]
    f32 = jnp.float32
    per_rep = pb.shape[1]
    slots = res.shape[0]
    off_pairs = n * (n - 1) // 2
    numbers = off_pairs + -(-n // 2)
    half = s_ref.shape[2] // 2
    width = s_ref.shape[3]
    piece = v.shape[2]
    same, swapped_rows, packed_first, packed_second = row_orders(size)

    def reorder(matrix, block):
        return jnp.dot(matrix.astype(jnp.bfloat16), block, preferred_element_type=f32)
    half_width = min(-(-width // 256) * 128, width)
    r, z, p = lax.axis_index("row"), lax.axis_index("col"), lax.axis_index("rep")

    def remote(src, dst, send, recv, **where):
        target = {"row": r, "col": z, "rep": p, **where}
        return pltpu.make_async_remote_copy(
            src_ref=src, dst_ref=dst, send_sem=send, recv_sem=recv,
            device_id=(target["row"], target["col"], target["rep"]), device_id_type=MESH)

    fetch = pltpu.make_async_copy(a_hbm, a_ref, la)
    fetch.start()

    barrier = pltpu.get_barrier_semaphore()

    def greet(**where):
        target = {"row": r, "col": z, "rep": p, **where}
        pl.semaphore_signal(
            barrier, inc=1, device_id=(target["row"], target["col"], target["rep"]),
            device_id_type=MESH)

    for off in range(1, n):
        greet(row=lax.rem(r + off, n))
    for off in range(1, reps):
        greet(rep=lax.rem(p + off, reps))

    @pl.when(z > 0)
    def _():
        greet(col=lax.max(z - 1, 0))

    @pl.when(z < n - 1)
    def _():
        greet(col=lax.min(z + 1, n - 1))

    def shuffle(k, off):
        dest = lax.rem(r + off, n)
        return remote(s_ref.at[dest, k], x.at[k, z, r], a_send.at[k, off - 1],
                      a_recv.at[k, off - 1], row=dest)

    def shuffled(k, off):
        source = lax.rem(r + n - off, n)
        return remote(s_ref.at[source, k], x.at[k, z, source], a_send.at[k, off - 1],
                      a_recv.at[k, off - 1], row=source)

    def stage(k):
        natural = jnp.concatenate([a_ref[i, k].astype(f32) for i in range(size)], axis=0)
        order = jnp.where(r < z, same, jnp.where(r > z, swapped_rows, same - swapped_rows))
        staged = reorder(order, natural.astype(s_ref.dtype)).astype(s_ref.dtype)
        for dest in range(n):
            start = dest * piece // 128 * 128
            stop = min(start + width, staged.shape[1])
            if stop - start < width:
                s_ref[dest, k, :, pl.ds(width - 256, 256)] = jnp.zeros(
                    (size * size, 256), s_ref.dtype)
            s_ref[dest, k, :, pl.ds(0, stop - start)] = staged[:, start:stop]

    acc[...] = jnp.zeros_like(acc)
    fetch.wait()
    stage(0)
    if reps * per_rep != numbers:
        dd[...] = jnp.zeros_like(dd)
    beside = (z > 0).astype(jnp.int32) + (z < n - 1).astype(jnp.int32)
    pl.semaphore_wait(barrier, n - 1 + reps - 1 + beside)
    def send_shuffle(k):
        for off in range(1, n):
            shuffle(k, off).start()
        x[k, z, r] = s_ref[r, k]

    send_shuffle(0)
    if kb > 1:
        stage(1)
        send_shuffle(1)

    left, right = lax.max(z - 1, 0), lax.min(z + 1, n - 1)

    def to_left(k, c):
        part = x.at[k, c, pl.ds(0, c)]
        return remote(part, part, l_send.at[k, c], x_recv.at[k, c], col=left)

    def to_right(k, c):
        part = x.at[k, c, pl.ds(c + 1, n - 1 - c)]
        return remote(part, part, r_send.at[k, c], x_recv.at[k, c], col=right)

    def diagonal(m, c):
        return g.at[c, m] if 2 * m + 1 < kb else g.at[c, m, :, pl.ds(0, half_width)]

    def g_left(m, c):
        return remote(diagonal(m, c), diagonal(m, c), gl_send.at[m, c], g_recv.at[m, c], col=left)

    def g_right(m, c):
        return remote(diagonal(m, c), diagonal(m, c), gr_send.at[m, c], g_recv.at[m, c], col=right)

    def pack(m):
        first = pack_rows(x[2 * m, z, z].astype(jnp.float32), size)
        if 2 * m + 1 < kb:
            second = pack_rows(x[2 * m + 1, z, z].astype(jnp.float32), size)
            g[z, m] = jnp.concatenate([first, second], axis=0).astype(g.dtype)
        else:
            tail = first[:, half_width:]
            if 2 * half_width > width:
                fill = jnp.zeros((half, 2 * half_width - width), jnp.float32)
                tail = jnp.concatenate([tail, fill], axis=1)
            g[z, m, :, pl.ds(0, half_width)] = jnp.concatenate(
                [first[:, :half_width], tail], axis=0).astype(g.dtype)

    def unpacked(k, c):
        m = k // 2
        if 2 * m + 1 < kb:
            both = g[c, m].astype(jnp.float32)
            return both[:half] if k % 2 == 0 else both[half:]
        both = g[c, m, :, pl.ds(0, half_width)].astype(jnp.float32)
        return jnp.concatenate([both[:half], both[half:, : width - half_width]], axis=1)

    for k in range(kb):
        for off in range(1, n):
            shuffled(k, off).wait_recv()
        for c in range(n):
            @pl.when(z == c)
            def _():
                if c > 0:
                    to_left(k, c).start()
                if c < n - 1:
                    to_right(k, c).start()
        pltpu.make_async_copy(v_hbm.at[k], v.at[k], lv.at[k]).start()
        if k + 2 < kb:
            stage(k + 2)
            send_shuffle(k + 2)
        if k % 2 == 1 or k == kb - 1:
            pack(k // 2)
            for c in range(n):
                @pl.when(z == c)
                def _():
                    if c > 0:
                        g_left(k // 2, c).start()
                    if c < n - 1:
                        g_right(k // 2, c).start()

    def slot_of(number):
        return number % reps * per_rep + number // reps

    def assemble(k, first, second):
        slot = slot_of(pair_start(first, n) + second - first - 1)

        @pl.when(z <= first)
        def _():
            dd[slot] = x[k, second, first]

        @pl.when(z >= second)
        def _():
            dd[slot] = x[k, first, second]

        @pl.when((z > first) & (z < second))
        def _():
            dd[slot] = (x[k, second, first].astype(f32)
                        - x[k, first, second].astype(f32)).astype(dd.dtype)

    def arrivals(k, d):
        for c in range(n):
            if c >= d:
                @pl.when(z == c - d)
                def _():
                    to_left(k, c).wait_recv()
                    x[k, c, c - d] = (x[k, c, c - d].astype(f32)
                                      - x[k, c - d, c].astype(f32)).astype(x.dtype)
                    if c > d:
                        to_left(k, c).start()
                    for m in range(-(-kb // 2)):
                        @pl.when(k == 2 * m)
                        def _():
                            g_left(m, c).wait_recv()
                            if c > d:
                                g_left(m, c).start()
            if c + d < n:
                @pl.when(z == c + d)
                def _():
                    to_right(k, c).wait_recv()
                    x[k, c, c + d] = (x[k, c + d, c].astype(f32)
                                      - x[k, c, c + d].astype(f32)).astype(x.dtype)
                    if c + d < n - 1:
                        to_right(k, c).start()
                    for m in range(-(-kb // 2)):
                        @pl.when(k == 2 * m)
                        def _():
                            g_right(m, c).wait_recv()
                            if c + d < n - 1:
                                g_right(m, c).start()

    def multiply(k):
        @pl.loop(0, n - 1)
        def _(first):
            @pl.loop(first + 1, n)
            def _(second):
                assemble(k, first, second)

        for now in range(kb):
            @pl.when(k == now)
            def _():
                for c in range(0, n, 2):
                    one = unpacked(now, c)
                    two = unpacked(now, c + 1) if c + 1 < n else jnp.zeros_like(one)
                    dd[slot_of(off_pairs + c // 2)] = jnp.concatenate(
                        [one, two], axis=0).astype(dd.dtype)

        pltpu.make_async_copy(v_hbm.at[k], v.at[k], lv.at[k]).wait()
        wide = dd[...].reshape(acc.shape[0], width).astype(f32)
        shift = lax.rem(width - lax.rem(r * piece, 128), width)
        aligned = pltpu.roll(wide, shift, 1)[:, :piece].astype(dd.dtype)
        acc[...] += lax.dot_general(
            aligned, v[k],
            (((1,), (1,)), ((), ())), preferred_element_type=f32)

    last = lax.max(z, n - 1 - z)
    for d in range(1, n):
        @pl.loop(0, kb)
        def _(k):
            arrivals(k, d)
            if 2 * d >= n - 1:
                @pl.when(d == last)
                def _():
                    multiply(k)

    pb[...] = acc[...].reshape(pb.shape).astype(pb.dtype)

    def swap_reps(off):
        other = lax.rem(p + off, reps)
        return remote(pb.at[other], rrecv.at[off - 1], p_send.at[off - 1], p_recv.at[off - 1],
                      rep=other)

    for off in range(1, reps):
        swap_reps(off).start()
    for off in range(1, reps):
        swap_reps(off).wait_recv()

    flip = lax.rem(p, 2)

    def owner(q):
        return lax.rem(q, n) * (1 - 2 * flip) + (n - 1) * flip

    def to_owner(q):
        return remote(qb.at[q], rowrecv.at[q // n, r], q_send.at[q],
                      q_recv.at[q // n, r], row=owner(q))

    for q in range(per_rep):
        total = pb[p, q].astype(jnp.float32)
        for off in range(1, reps):
            total += rrecv[off - 1, q].astype(jnp.float32)
        qb[q] = total.astype(qb.dtype)

        @pl.when(owner(q) != r)
        def _():
            to_owner(q).start()

    mine = r * (1 - 2 * flip) + (n - 1) * flip

    place = lax.broadcasted_iota(jnp.int32, (size * size, 128), 0)
    place_i = sum((place >= t * size).astype(jnp.int32) for t in range(1, size))
    place_j = place - size * place_i
    target = jnp.bitwise_xor(slab_ref[0], slab_ref[1])

    def labels(orbitals):
        return sum((orbitals >= occ_ref[t]).astype(jnp.int32)
                   for t in range(1, occ_ref.shape[0] - 1))

    def masked(block, first, second):
        mixed = jnp.bitwise_xor(labels(first * size + place_i), labels(second * size + place_j))
        allowed = (mixed == target).astype(f32)[:, :1]
        return jnp.where(jnp.broadcast_to(allowed, block.shape) > 0, block, jnp.zeros_like(block))

    def number_of(s):
        return (s * n + mine) * reps + p

    def blocks_of(s):
        number = number_of(s)
        first = 0
        for t in range(1, n - 1):
            first = first + (number >= pair_start(t, n)).astype(jnp.int32)
        second = number - pair_start(first, n) + first + 1
        even = 2 * (number - off_pairs)
        apart = number < off_pairs
        first, other = jnp.where(apart, first, even), jnp.where(apart, first, even + 1)
        second, swapped = jnp.where(apart, second, even), jnp.where(apart, second, even + 1)
        return first, second, other, swapped

    def deliver(s, do):
        first, second, other, swapped = blocks_of(s)
        for rep in range(reps):
            for t, (row, col) in enumerate(((first, second), (swapped, other))):
                local = (row == r) & (col == z) & (p == rep)
                wanted = (row < n) & (col < n)

                @pl.when(wanted & local)
                def _():
                    if do == "start":
                        pltpu.make_async_copy(res.at[s, t], found.at[z], o_recv.at[z]).start()

                @pl.when(wanted & jnp.logical_not(local))
                def _():
                    copy = remote(res.at[s, t], found.at[z], o_send.at[s, rep, t],
                                  o_recv.at[z], row=row, col=col, rep=rep)
                    if do == "start":
                        copy.start()
                    else:
                        copy.wait_send()

    for s in range(slots):
        @pl.when((s * n + mine < per_rep) & (number_of(s) < numbers))
        def _():
            total = qb[s * n + mine].astype(jnp.float32)
            for off in range(1, n):
                source = lax.rem(r + off, n)
                remote(rowrecv.at[s, source], rowrecv.at[s, source], q_send.at[0],
                       q_recv.at[s, source], row=source).wait_recv()
                total += rowrecv[s, source].astype(jnp.float32)

            first, second, other, swapped = blocks_of(s)
            apart = number_of(s) < off_pairs
            rounded = total.astype(res.dtype)
            one = reorder(jnp.where(apart, same, packed_first), rounded)
            two = reorder(jnp.where(apart, -swapped_rows, packed_second), rounded)
            res[s, 0] = masked(one, first, second).astype(res.dtype)
            res[s, 1] = masked(two, swapped, other).astype(res.dtype)
            deliver(s, "start")

    for source in range(n):
        remote(found.at[source], found.at[source], o_send.at[0, 0, 0], o_recv.at[source],
               col=source).wait_recv()

    whole = jnp.concatenate([found[source].astype(f32) for source in range(n)], axis=1)
    for i in range(size):
        out_ref[i] = -whole[i * size : (i + 1) * size].astype(out_ref.dtype)

    for s in range(slots):
        @pl.when((s * n + mine < per_rep) & (number_of(s) < numbers))
        def _():
            deliver(s, "wait")
    for q in range(per_rep):
        @pl.when(owner(q) != r)
        def _():
            to_owner(q).wait_send()
    for off in range(1, reps):
        swap_reps(off).wait_send()

    @pl.loop(0, kb)
    def _(k):
        for off in range(1, n):
            shuffle(k, off).wait_send()
        for c in range(n):
            if c > 0:
                @pl.when((z <= c) & (z > 0))
                def _():
                    to_left(k, c).wait_send()
            if c < n - 1:
                @pl.when((z >= c) & (z < n - 1))
                def _():
                    to_right(k, c).wait_send()

    for m in range(-(-kb // 2)):
        for c in range(n):
            if c > 0:
                @pl.when((z <= c) & (z > 0))
                def _():
                    g_left(m, c).wait_send()
            if c < n - 1:
                @pl.when((z >= c) & (z < n - 1))
                def _():
                    g_right(m, c).wait_send()


def ladder_blocks(amplitudes, integrals, occ_offsets, slab, n, reps):
    size, kb, _, pairs = amplitudes.shape
    rows, piece = size * size, pairs // n
    width = max(-(-(t * piece % 128 + piece) // 128) * 128 for t in range(n))
    slab_rows = integrals.shape[1]
    numbers = n * (n - 1) // 2 + -(-n // 2)
    chunks = -(-kb // 2)
    per_rep = -(-numbers // reps)
    slots = -(-per_rep // n)
    bf16, dma = jnp.bfloat16, pltpu.SemaphoreType.DMA
    return pl.pallas_call(
        functools.partial(kernel, n, reps, size),
        out_shape=jax.ShapeDtypeStruct((size, size, n * slab_rows), bf16),
        in_specs=[
            pl.BlockSpec(memory_space=pl.ANY),
            pl.BlockSpec(memory_space=pl.ANY),
            pl.BlockSpec(memory_space=pltpu.SMEM),
            pl.BlockSpec(memory_space=pltpu.SMEM),
        ],
        out_specs=pl.BlockSpec(memory_space=pltpu.VMEM),
        scratch_shapes=[
            pltpu.VMEM(amplitudes.shape[:1] + (kb, size, pairs), bf16),
            pltpu.VMEM((n, kb, rows, width), bf16),
            pltpu.VMEM((n, rows, slab_rows), bf16),
            pltpu.VMEM((kb, n, n, rows, width), bf16),
            pltpu.VMEM((n, chunks, rows, width), bf16),
            pltpu.VMEM((reps * per_rep, rows, width), bf16),
            pltpu.VMEM((kb, slab_rows, piece), bf16),
            pltpu.VMEM((reps * per_rep * rows, slab_rows), jnp.float32),
            pltpu.VMEM((reps, per_rep, rows, slab_rows), bf16),
            pltpu.VMEM((max(reps - 1, 1), per_rep, rows, slab_rows), bf16),
            pltpu.VMEM((per_rep, rows, slab_rows), bf16),
            pltpu.VMEM((slots, n, rows, slab_rows), bf16),
            pltpu.VMEM((slots, 2, rows, slab_rows), bf16),
            dma,
            dma((kb,)),
            dma((kb, n - 1)),
            dma((kb, n - 1)),
            dma((kb, n)),
            dma((kb, n)),
            dma((kb, n)),
            dma((chunks, n)),
            dma((chunks, n)),
            dma((chunks, n)),
            dma((max(reps - 1, 1),)),
            dma((max(reps - 1, 1),)),
            dma((per_rep,)),
            dma((slots, n)),
            dma((slots, reps, 2)),
            dma((n,)),
        ],
        compiler_params=pltpu.CompilerParams(
            collective_id=0, has_side_effects=True, vmem_limit_bytes=56 * 1024 * 1024),
        name="ladder_blocks",
    )(amplitudes, integrals, occ_offsets, slab)


def shards(n, reps, amplitudes, integrals, occ_offsets, slab):
    return -ladder_blocks(
        jnp.transpose(amplitudes, (0, 2, 1, 3)), jnp.transpose(integrals, (1, 0, 2)),
        occ_offsets, slab, n, reps)


def solution(mesh):
    placed = (P("row", "col", "rep", None), P("col", "rep", "row"), P(), P())
    n, reps = mesh.shape["row"], mesh.shape["rep"]
    assert mesh.shape["col"] == n
    return jax.shard_map(
        functools.partial(shards, n, reps), mesh=mesh, in_specs=placed,
        out_specs=P("row", "col", None), check_vma=False
    )
```
